256 devices in a mesh: rows: 32 (over z, y), cols: 8 (over x, core).
Axes of the slice: x: 4, y: 4, z: 8, core: 2. Of those that a mesh axis runs over, the one named last changes fastest.
Arguments:
- genotypes: float32 [294912, 2048], P('rows', 'cols'), as said below
- right_sides: float32 [294912, 64], P(('rows', 'cols')), may hold values from -6 to 6
- inverse_r: float32 [2048, 2048], P('cols'), as said below
Outputs:
- solution: float32 [2048, 64], P('cols')
- last_basis: float32 [294912, 64], P(('rows', 'cols'))
The draws below stay inside these ranges and needn't reach their ends.
Inputs may be any that keep to these rules, and one draw needn't show every extreme that they name: `genotypes`: each column is a genotype count of 0, 1 or 2, centred by its allele frequency and scaled per column. `inverse_r`: upper triangular with a diagonal between 1 and 2.
All inputs are finite; a program needn't handle non-finite values.
Results may differ from the reference program's by a relative error of at most 0.0003.
Values sent between devices are 32-bit elements; how exact they have to be, the bound alone decides.
A program may use at most 64 MiB of HBM per device.

```python
import math
import jax
import jax.numpy as jnp
from jax import lax

N = 2048
K = 64
ITERS = 2
SAMPLES = 294912


def draw_genotypes(key, part):
    key = jax.random.fold_in(key, 7)
    first_key, second_key = jax.random.split(key, 2)
    frequency = jax.random.uniform(first_key, (1, N), jnp.float32, 0.05, 0.5)
    uniform_draw = jax.random.uniform(second_key, (SAMPLES, N), jnp.float32)
    counts = (uniform_draw < 2.0 * frequency - frequency * frequency).astype(jnp.float32) + (uniform_draw < frequency * frequency).astype(jnp.float32)
    values = (counts - 2.0 * frequency) / jnp.sqrt(2.0 * frequency * (1.0 - frequency))
    return values


def draw_inverse_r(key, part):
    key = jax.random.fold_in(key, 11)
    first_key, second_key = jax.random.split(key)
    positions = jnp.arange(N)
    strictly_upper = (positions[None, :] > positions[:, None]).astype(jnp.float32)
    diagonal = jax.random.uniform(first_key, (N,), jnp.float32, 1.0, 2.0)
    spread = jax.random.normal(second_key, (N, N), jnp.float32) * 0.5
    return spread * strictly_upper / math.sqrt(N) + jnp.diag(diagonal)


def levels(own_key, shape, cuts, low, high):
    level = 1.0
    for axis_at, blocks in cuts:
        heights = jax.random.uniform(jax.random.fold_in(jax.random.fold_in(own_key, 6), axis_at), (blocks,), jnp.float32, low / len(cuts), high / len(cuts))
        level = level * jnp.repeat(jnp.exp(heights), shape[axis_at] // blocks).reshape((-1,) + (1,) * (len(shape) - 1 - axis_at))
    return level


def bell_draw(key, dims, deviation, most, cuts=(), kind=jnp.bfloat16):
    array = jax.random.normal(key, dims, jnp.float32) * deviation
    if len(cuts) > 0:
        array = levels(key, dims, cuts, -0.22, 0.18) * array
    return jnp.clip(array, min=-most, max=most).astype(kind)


def setup_inputs(seed: int = 0) -> dict:
    key_list = jax.random.split(jax.random.key(seed), 4)
    genotypes = draw_genotypes(jax.random.fold_in(key_list[3], 71), 0)
    right_sides = bell_draw(key_list[1], (SAMPLES, K), 1.0, 6.0, ((0, 256),), jnp.float32)
    inverse_r = draw_inverse_r(jax.random.fold_in(key_list[3], 71), 0)
    return {"genotypes": genotypes, "right_sides": right_sides, "inverse_r": inverse_r}


def product(left, right):
    return jnp.dot(left.astype(jnp.float32), right.astype(jnp.float32), precision=lax.Precision.HIGHEST, preferred_element_type=jnp.float32)

def orthonormal(lower_factor, block):
    return jax.scipy.linalg.solve_triangular(lower_factor, block.T, lower=True).T

def small_solution(alphas, betas, block_width):
    steps_count = len(alphas)
    bidiagonal = jnp.zeros(((steps_count + 1) * block_width, steps_count * block_width), jnp.float32)
    for position in range(steps_count):
        low = position * block_width
        bidiagonal = bidiagonal.at[low:low + block_width, low:low + block_width].set(alphas[position].T)
        bidiagonal = bidiagonal.at[low + block_width:low + 2 * block_width, low:low + block_width].set(betas[position + 1])
    normal_matrix = product(bidiagonal.T, bidiagonal)
    target = jnp.zeros((steps_count * block_width, block_width), jnp.float32)
    target = target.at[:block_width].set(product(alphas[0], betas[0]))
    factor = jnp.linalg.cholesky(normal_matrix)
    return jax.scipy.linalg.cho_solve((factor, True), target)

def reference(genotypes, right_sides, inverse_r):
    block_width = right_sides.shape[1]
    lower_factor = jnp.linalg.cholesky(product(right_sides.T, right_sides))
    betas = [lower_factor.T]
    basis = orthonormal(lower_factor, right_sides)
    alphas = []
    directions = []
    for iteration in range(ITERS):
        image = product(inverse_r.T, product(genotypes.T, basis))
        if iteration > 0:
            image = image - product(directions[-1], betas[-1].T)
        lower_factor = jnp.linalg.cholesky(product(image.T, image))
        alphas.append(lower_factor.T)
        directions.append(orthonormal(lower_factor, image))
        mapped = product(genotypes, product(inverse_r, directions[-1])) - product(basis, alphas[-1].T)
        lower_factor = jnp.linalg.cholesky(product(mapped.T, mapped))
        betas.append(lower_factor.T)
        basis = orthonormal(lower_factor, mapped)
    coefficients = small_solution(alphas, betas, block_width)
    combined = jnp.zeros(directions[0].shape, jnp.float32)
    for position in range(ITERS):
        combined = combined + product(directions[position], coefficients[position * block_width:(position + 1) * block_width])
    return (product(inverse_r, combined), basis)
```

```python
import functools

import jax
import jax.numpy as jnp
from jax import lax
from jax.experimental import pallas as pl
from jax.experimental.pallas import tpu as pltpu
from jax.sharding import PartitionSpec as P

F32 = jnp.float32
BF16 = jnp.bfloat16
NN = (((1,), (0,)), ((), ()))
NT = (((1,), (1,)), ((), ()))
CHIPS = 4
CORES = 2
PEERS = CHIPS * CORES
SCALE = 4096.0


def exact(left, right, dims=NN):
    return lax.dot_general(
        left, right, dims, precision=lax.Precision.HIGHEST, preferred_element_type=F32
    )


def parts(value):
    high = value.astype(BF16)
    return high, (value - high.astype(F32)).astype(BF16)


def three_pass(value, high, low, dims):
    rows = value.shape[0]
    v_high, v_low = parts(value)
    both = lax.dot_general(
        jnp.concatenate([v_high, v_low], axis=0), high, dims, preferred_element_type=F32
    )
    return (
        both[:rows]
        + both[rows:]
        + lax.dot_general(v_high, low, dims, preferred_element_type=F32)
    )


def doubled(rows):
    return jnp.concatenate([rows, rows], axis=0)


def iotas(size):
    row = lax.broadcasted_iota(jnp.int32, (size, 2 * size), 0)
    lane = lax.broadcasted_iota(jnp.int32, (size, 2 * size), 1)
    return row, lane


def with_identity(twice):
    size = twice.shape[0]
    row, lane = iotas(size)
    return jnp.where(lane < size, jnp.where(lane == row, 1.0, 0.0), twice)


def eliminate(systems, full):
    size = systems[0].shape[0]
    row_at, _ = iotas(size)
    systems = list(systems)
    for j in range(size):
        for i, m in enumerate(systems):
            column = m[:, size + j : size + j + 1]
            row = m[j : j + 1, :] * (1.0 / m[j : j + 1, size + j : size + j + 1])
            if full[i]:
                systems[i] = jnp.where(row_at == j, row, m - column * row)
            else:
                systems[i] = jnp.where(row_at > j, m - column * row, m)
    return systems


def inverse(twice):
    size = twice.shape[0]
    return eliminate([with_identity(twice)], [True])[0][:, :size]


def diagonal(twice):
    size = twice.shape[0]
    row, lane = iotas(size)
    as_column = jnp.sum(jnp.where(lane == row, twice, 0.0), axis=1, keepdims=True)
    hit = jnp.logical_or(lane == row, lane == row + size)
    as_row = jnp.sum(jnp.where(hit, twice, 0.0), axis=0, keepdims=True)
    return as_column, as_row


class Net:
    def __init__(self, send_sems, recv_sems):
        self.send_sems, self.recv_sems = send_sems, recv_sems
        self.sent = []

    def send(self, source, target, **device):
        at = len(self.sent)
        copy = pltpu.make_async_remote_copy(
            src_ref=source,
            dst_ref=target,
            send_sem=self.send_sems.at[at],
            recv_sem=self.recv_sems.at[at],
            device_id=device,
            device_id_type=pl.DeviceIdType.MESH,
        )
        copy.start()
        self.sent.append(copy)
        return copy

    def finish(self):
        for copy in self.sent:
            copy.wait_send()


def body(
    nz, ny,
    g_hbm, b_ref, p_ref, u_ref, s_ref,
    g_f32, g_high, g_low, p_high, p_low,
    b_full, n_full, i_full, j_full, j_out,
    y_part, y_sib, y_fwd, y_left, y_right,
    t_part, t_sib, t_fwd, t_left, t_right,
    az, zbuf, ybuf,
    sm_own, sm_x, sm_z, sm_y, sm_out,
    g_sems, send_sems, recv_sems,
):
    width, rows_w = b_ref.shape
    block = p_ref.shape[0]
    half = width // 2
    r, c = lax.axis_index("rows"), lax.axis_index("cols")
    x, k = c // CORES, c % CORES
    z, y = r // ny, r % ny
    right = lax.rem(x + 1, CHIPS)
    left = lax.rem(x + CHIPS - 1, CHIPS)
    opposite = lax.rem(x + 2, CHIPS)
    c_sib = x * CORES + 1 - k
    c_right, c_left, c_opp = (chip * CORES + k for chip in (right, left, opposite))
    net = Net(send_sems, recv_sems)

    def chunk(at):
        return pl.ds(pl.multiple_of(at * rows_w, rows_w), rows_w)

    loads = []
    for step, at in enumerate((c, c_sib, c_left, c_right, c_left + 1 - 2 * k, c_right + 1 - 2 * k, c_opp, c_opp + 1 - 2 * k)):
        copy = pltpu.make_async_copy(g_hbm.at[chunk(at)], g_f32.at[chunk(at)], g_sems.at[step])
        copy.start()
        loads.append(copy)

    barrier = pltpu.get_barrier_semaphore()
    greeted = 0
    for d in range(1, PEERS):
        pl.semaphore_signal(barrier, inc=1, device_id={"cols": lax.rem(c + d, PEERS)}, device_id_type=pl.DeviceIdType.MESH)
        greeted += 1
    for d in range(1, nz):
        pl.semaphore_signal(barrier, inc=1, device_id={"rows": lax.rem(z + d, nz) * ny + y}, device_id_type=pl.DeviceIdType.MESH)
        greeted += 1
    for d in range(1, ny):
        pl.semaphore_signal(barrier, inc=1, device_id={"rows": z * ny + lax.rem(y + d, ny)}, device_id_type=pl.DeviceIdType.MESH)
        greeted += 1
    b_full[c] = b_ref[...]
    pl.semaphore_wait(barrier, greeted)

    upper, lower = pl.ds(0, half), pl.ds(half, half)

    def gather(full, on_block):
        def copy_to(at, rows, target):
            return net.send(full.at[at, rows], full.at[at, rows], cols=target)

        right_upper = copy_to(c, upper, c_right)
        left_lower = copy_to(c, lower, c_left)
        right_lower = copy_to(c, lower, c_right)
        left_upper = copy_to(c, upper, c_left)
        sib_own = net.send(full.at[c], full.at[c], cols=c_sib)
        on_block(c, 0)
        right_upper.wait_recv()
        onward_right = copy_to(c_left, upper, c_right)
        sib_left_upper = copy_to(c_left, upper, c_sib)
        left_lower.wait_recv()
        onward_left = copy_to(c_right, lower, c_left)
        sib_right_lower = copy_to(c_right, lower, c_sib)
        sib_own.wait_recv()
        on_block(c_sib, 1)
        right_lower.wait_recv()
        sib_left_lower = copy_to(c_left, lower, c_sib)
        left_upper.wait_recv()
        sib_right_upper = copy_to(c_right, upper, c_sib)
        on_block(c_left, 2)
        on_block(c_right, 3)
        sib_left_upper.wait_recv()
        sib_left_lower.wait_recv()
        on_block(c_left + 1 - 2 * k, 4)
        sib_right_lower.wait_recv()
        sib_right_upper.wait_recv()
        on_block(c_right + 1 - 2 * k, 5)
        onward_right.wait_recv()
        sib_opp_upper = copy_to(c_opp, upper, c_sib)
        onward_left.wait_recv()
        sib_opp_lower = copy_to(c_opp, lower, c_sib)
        on_block(c_opp, 6)
        sib_opp_upper.wait_recv()
        sib_opp_lower.wait_recv()
        on_block(c_opp + 1 - 2 * k, 7)

    def scatter(compute, part, sib, fwd, from_left, from_right, beside=None):
        def pair(chip, slot):
            mine, theirs = chip * CORES + k, chip * CORES + 1 - k
            part[theirs] = compute(theirs)
            copy = net.send(part.at[theirs], sib.at[slot], cols=c_sib)
            part[mine] = compute(mine)
            return copy

        sib_opp = pair(opposite, 0)
        sib_right = pair(right, 1)
        sib_opp.wait_recv()
        part[c_opp] = part[c_opp] + sib[0]
        fwd_upper = net.send(part.at[c_opp, upper], fwd.at[upper], cols=c_right)
        fwd_lower = net.send(part.at[c_opp, lower], fwd.at[lower], cols=c_left)
        sib_left = pair(left, 2)
        sib_right.wait_recv()
        part[c_right] = part[c_right] + sib[1]
        right_lower = net.send(part.at[c_right, lower], from_left.at[lower], cols=c_right)
        sib_own = pair(x, 3)
        sib_left.wait_recv()
        part[c_left] = part[c_left] + sib[2]
        left_upper = net.send(part.at[c_left, upper], from_right.at[upper], cols=c_left)
        fwd_upper.wait_recv()
        part[c_right, upper] = part[c_right, upper] + fwd[upper]
        right_upper = net.send(part.at[c_right, upper], from_left.at[upper], cols=c_right)
        fwd_lower.wait_recv()
        part[c_left, lower] = part[c_left, lower] + fwd[lower]
        left_lower = net.send(part.at[c_left, lower], from_right.at[lower], cols=c_left)
        extra = beside() if beside is not None else None
        sib_own.wait_recv()
        total = part[c] + sib[3]
        for copy in (right_lower, left_upper, right_upper, left_lower):
            copy.wait_recv()
        return total + from_left[...] + from_right[...], extra

    share = width // nz

    def sum_rows(value, at, full):
        own, zb, yb = az.at[at], zbuf.at[at], ybuf.at[at]
        own[...] = value
        copies = []
        for d in range(1, nz):
            to = lax.rem(z + d, nz)
            copies.append(net.send(own.at[pl.ds(pl.multiple_of(to * share, share), share)], zb.at[d - 1], rows=to * ny + y))
        mine = pl.ds(pl.multiple_of(z * share, share), share)
        total = own[mine]
        for d in range(1, nz):
            copies[d - 1].wait_recv()
            total = total + zb[d - 1]
        yb[y] = total
        copies = [
            net.send(yb.at[y], yb.at[y], rows=z * ny + lax.rem(y + d, ny)) for d in range(1, ny)
        ]
        for copy in copies:
            copy.wait_recv()
        total = yb[0]
        for i in range(1, ny):
            total = total + yb[i]
        full[c, mine] = total
        copies = [
            net.send(full.at[c, mine], full.at[c, mine], rows=lax.rem(z + d, nz) * ny + y) for d in range(1, nz)
        ]
        for copy in copies:
            copy.wait_recv()

    def small_sum(value, at):
        piece = width // PEERS
        own, xb, zb, yb, out = sm_own.at[at], sm_x.at[at], sm_z.at[at], sm_y.at[at], sm_out.at[at]
        own[...] = value
        copies = []
        for d in range(1, PEERS):
            to = lax.rem(c + d, PEERS)
            copies.append(net.send(own.at[pl.ds(pl.multiple_of(to * piece, piece), piece)], xb.at[d - 1], cols=to))
        yield
        mine = pl.ds(pl.multiple_of(c * piece, piece), piece)
        total = own[mine]
        for d in range(1, PEERS):
            copies[d - 1].wait_recv()
            total = total + xb[d - 1]
        zb[z] = total
        copies = [
            net.send(zb.at[z], zb.at[z], rows=lax.rem(z + d, nz) * ny + y) for d in range(1, nz)
        ]
        yield
        for copy in copies:
            copy.wait_recv()
        total = zb[0]
        for i in range(1, nz):
            total = total + zb[i]
        yb[y] = total
        copies = [
            net.send(yb.at[y], yb.at[y], rows=z * ny + lax.rem(y + d, ny)) for d in range(1, ny)
        ]
        yield
        for copy in copies:
            copy.wait_recv()
        total = yb[0]
        for i in range(1, ny):
            total = total + yb[i]
        out[mine] = total
        copies = [
            net.send(out.at[mine], out.at[mine], cols=lax.rem(c + d, PEERS)) for d in range(1, PEERS)
        ]
        yield
        for copy in copies:
            copy.wait_recv()
        yield

    def backward(full, first=None):
        totals = [None]

        def on_block(at, step):
            if first is not None:
                first(at, step)
            term = three_pass(full[at], g_high[chunk(at)], g_low[chunk(at)], NN)
            totals[0] = term if totals[0] is None else totals[0] + term

        gather(full, on_block)
        return totals[0]

    def transpose_applied(value, at, full):
        def compute(j):
            lanes = pl.ds(pl.multiple_of(j * block, block), block)
            return three_pass(value, p_high[:, lanes], p_low[:, lanes], NN)

        total, _ = scatter(compute, t_part.at[at], t_sib.at[at], t_fwd.at[at], t_left.at[at], t_right.at[at])
        sum_rows(total, at, full)
        gather(full, lambda *_: None)

    def applied(full):
        total = None
        for j in range(PEERS):
            lanes = pl.ds(j * block, block)
            term = three_pass(full[j], p_high[:, lanes], p_low[:, lanes], NT)
            total = term if total is None else total + term
        return total

    def forward(value, at, beside):
        def compute(j):
            return three_pass(value, g_high[chunk(j)], g_low[chunk(j)], NT)

        return scatter(compute, y_part.at[at], y_sib.at[at], y_fwd.at[at], y_left.at[at], y_right.at[at], beside)

    def gram(left, right):
        total = None
        for j in range(PEERS):
            term = exact(left[j], doubled(right[j]), NT)
            total = term if total is None else total + term
        return total

    b_own = b_ref[...]
    sums = small_sum(exact(b_own, doubled(b_own), NT), 0)

    def load(at, step):
        loads[step].wait()
        high, low = parts(g_f32[chunk(at)])
        g_high[chunk(at)] = high
        g_low[chunk(at)] = low
        if step in (0, 1, 3, 5, 6):
            next(sums)

    p_high[...], p_low[...] = parts(p_ref[...])
    summed = backward(b_full, load)
    transpose_applied(summed, 0, i_full)
    x_one = applied(i_full)

    def beside_one():
        c_zero = gram(i_full, i_full)
        return c_zero, inverse(sm_out[0])

    y_one, (c_zero, gram_inverse) = forward(x_one, 0, beside_one)
    scale_one, scale_one_row = (lax.rsqrt(v) for v in diagonal(c_zero))
    c_one = c_zero[:, :width]
    left_one = exact(c_one, gram_inverse)
    n_one = scale_one * (y_one - exact(left_one, b_own))
    n_full[c] = n_one

    summed = backward(n_full)
    c_inverse = inverse(c_zero)
    transpose_applied(summed, 1, j_full)
    x_jay = applied(j_full)
    h_raw = gram(j_full, i_full)
    out_of = exact(h_raw[:, :width], c_inverse)
    x_two = x_jay - exact(out_of, x_one)

    def beside_two():
        for j in range(PEERS):
            j_out[j] = j_full[j] - exact(out_of, i_full[j])
        e_raw = gram(j_out, j_out)
        scale_two, scale_two_row = (lax.rsqrt(v) for v in diagonal(e_raw))
        h_one = h_raw * scale_one_row
        c_row = c_zero * scale_one_row
        normal = h_one + scale_one * exact(left_one, c_row)
        h_inv, s_inv = (
            m[:, :width]
            for m in eliminate([with_identity(h_one), with_identity(normal)], [True, True])
        )
        e_col = scale_two * e_raw[:, :width]
        e_row = e_raw * scale_two_row
        schur = exact(exact(e_col, h_inv - s_inv), e_row)
        d_t = exact(c_row[:, :width], s_inv)
        w = exact(d_t, e_row[:, :width])
        back = exact(exact(e_raw[:, :width], h_inv), n_one)
        return scale_two, e_col, c_row, s_inv, schur, w, back

    y_two, (scale_two, e_col, c_row, s_inv, schur, w, back) = forward(x_two, 1, beside_two)
    n_two = scale_two * (y_two - back)
    for _ in small_sum(exact(n_two, doubled(n_two), NT), 1):
        pass
    h_two = sm_out[1]
    lower_inv, last = eliminate(
        [with_identity(h_two), with_identity(h_two + schur)], [False, True]
    )
    row_at, lane_at = iotas(width)
    pivots = jnp.sum(jnp.where(lane_at == row_at + width, lower_inv, 0.0), axis=1, keepdims=True)
    u_ref[...] = exact(lax.rsqrt(pivots) * lower_inv[:, :width], n_two)
    b_t = -exact(w, last[:, :width])
    a_t = exact(c_row[:, :width] - exact(b_t, e_col), s_inv)
    s_ref[...] = SCALE * (exact(a_t, scale_one * x_one) + exact(b_t, scale_two * x_two))
    net.finish()


def solution(mesh, ny=4):
    nrows = mesh.shape["rows"]
    nz = nrows // ny

    def per_device(genotypes, right_sides, inverse_r):
        rows, block = genotypes.shape
        rows_w, width = right_sides.shape
        variants = inverse_r.shape[1]
        share = width // nz
        piece = width // PEERS
        v = pltpu.VMEM
        messages = 4 * 13 + 4 * 10 + 2 * (2 * (nz - 1) + ny - 1) + 2 * (2 * (PEERS - 1) + nz + ny - 2)
        u_t, s_t = pl.pallas_call(
            functools.partial(body, nz, ny),
            out_shape=(
                jax.ShapeDtypeStruct((width, rows_w), F32),
                jax.ShapeDtypeStruct((width, block), F32),
            ),
            in_specs=[
                pl.BlockSpec(memory_space=pl.ANY),
                pl.BlockSpec(memory_space=pltpu.VMEM),
                pl.BlockSpec(memory_space=pltpu.VMEM),
            ],
            out_specs=[pl.BlockSpec(memory_space=pltpu.VMEM)] * 2,
            scratch_shapes=[
                v((rows, block), F32), v((rows, block), BF16), v((rows, block), BF16),
                v((block, variants), BF16), v((block, variants), BF16),
                v((PEERS, width, rows_w), F32), v((PEERS, width, rows_w), F32),
                v((PEERS, width, block), F32), v((PEERS, width, block), F32), v((PEERS, width, block), F32),
                v((2, PEERS, width, rows_w), F32), v((2, CHIPS, width, rows_w), F32),
                v((2, width, rows_w), F32), v((2, width, rows_w), F32), v((2, width, rows_w), F32),
                v((2, PEERS, width, block), F32), v((2, CHIPS, width, block), F32),
                v((2, width, block), F32), v((2, width, block), F32), v((2, width, block), F32),
                v((2, width, block), F32), v((2, nz - 1, share, block), F32), v((2, ny, share, block), F32),
                v((2, width, 2 * width), F32), v((2, PEERS - 1, piece, 2 * width), F32),
                v((2, nz, piece, 2 * width), F32), v((2, ny, piece, 2 * width), F32),
                v((2, width, 2 * width), F32),
                pltpu.SemaphoreType.DMA((PEERS,)),
                pltpu.SemaphoreType.DMA((messages,)),
                pltpu.SemaphoreType.DMA((messages,)),
            ],
            compiler_params=pltpu.CompilerParams(
                collective_id=0, has_side_effects=True, vmem_limit_bytes=58 * 1024 * 1024
            ),
        )(genotypes, right_sides.T * (1.0 / SCALE), inverse_r)
        return s_t.T, u_t.T

    in_specs = (P("rows", "cols"), P(("rows", "cols"), None), P("cols", None))
    out_specs = (P("cols", None), P(("rows", "cols"), None))
    return jax.shard_map(
        per_device, mesh=mesh, in_specs=in_specs, out_specs=out_specs, check_vma=False
    )
```

```python
import functools

import jax
import jax.numpy as jnp
from jax import lax
from jax.experimental import pallas as pl
from jax.experimental.pallas import tpu as pltpu
from jax.sharding import PartitionSpec as P

F32 = jnp.float32
BF16 = jnp.bfloat16
NN = (((1,), (0,)), ((), ()))
NT = (((1,), (1,)), ((), ()))
CHIPS = 4
CORES = 2
PEERS = CHIPS * CORES
SCALE = 4096.0


def exact(left, right, dims=NN):
    return lax.dot_general(
        left, right, dims, precision=lax.Precision.HIGHEST, preferred_element_type=F32
    )


def dot(left, right, dims):
    return lax.dot_general(left, right, dims, preferred_element_type=F32)


def parts(value):
    high = value.astype(BF16).astype(F32)
    rest = value - high
    middle = rest.astype(BF16).astype(F32)
    return high, middle, rest - middle


def stacked_parts(value):
    rows = value.shape[0]
    stack = jnp.concatenate(parts(value), axis=0)
    if 3 * rows % 16:
        stack = jnp.concatenate([stack, jnp.zeros((16 - 3 * rows % 16, value.shape[1]), F32)], axis=0)
    return stack.astype(BF16)


def with_counts(value, counts, dims):
    rows = value.shape[0]
    out = dot(stacked_parts(value), counts, dims)
    return out[2 * rows : 3 * rows] + out[rows : 2 * rows] + out[:rows]


def with_parts(value, right, dims):
    rows = value.shape[0]
    stack = stacked_parts(value)
    first = dot(stack, right[0], dims)
    second = dot(stack[: max(2 * rows, 16)], right[1], dims)
    small = first[2 * rows : 3 * rows] + second[rows : 2 * rows]
    return small + (first[rows : 2 * rows] + second[:rows]) + first[:rows]


def doubled(rows):
    return jnp.concatenate([rows, rows], axis=0)


def iotas(rows, lanes):
    row = lax.broadcasted_iota(jnp.int32, (rows, lanes), 0)
    lane = lax.broadcasted_iota(jnp.int32, (rows, lanes), 1)
    return row, lane


def with_identity(twice):
    size = twice.shape[0]
    row, lane = iotas(size, 2 * size)
    return jnp.where(lane < size, jnp.where(lane == row, 1.0, 0.0), twice)


def eliminate(systems, full, done, stride=4):
    size = systems[0].shape[0]
    shape = (size, 2 * size)
    row_at, _ = iotas(*shape)
    systems = list(systems)
    for j in range(0, size, 2):
        for i, m in enumerate(systems):
            first = jnp.broadcast_to(m[:, size + j : size + j + 1], shape)
            second = jnp.broadcast_to(m[:, size + j + 1 : size + j + 2], shape)
            top, bottom = m[j : j + 1, :], m[j + 1 : j + 2, :]
            inverse = 1.0 / first[j : j + 1, :]
            ratio = first[j + 1 : j + 2, :] * inverse
            across = second[j : j + 1, :]
            pivot = 1.0 / (second[j + 1 : j + 2, :] - ratio * across)
            row_two = (bottom - ratio * top) * pivot
            row_one = (top - across * row_two) * inverse
            less = m - first * row_one - second * row_two
            if full[i]:
                systems[i] = jnp.where(row_at == j, row_one, jnp.where(row_at == j + 1, row_two, less))
            else:
                systems[i] = jnp.where(row_at > j + 1, less, m)
        if j // 2 % stride == stride - 1:
            yield
    done.extend(systems)


def factors(m):
    size = m.shape[0]
    row, lane = iotas(size, 2 * size)
    odd = lax.rem(row, 2) == 1
    above = pltpu.roll(m, 1, 0)
    left = jnp.logical_and(odd, lane == row + size - 1)
    under = jnp.sum(jnp.where(left, m, 0.0), axis=1, keepdims=True)
    over = jnp.sum(jnp.where(left, above, jnp.where(jnp.logical_and(lane == 0, jnp.logical_not(odd)), 1.0, 0.0)), axis=1, keepdims=True)
    m = m - (under / over) * above
    pivots = jnp.sum(jnp.where(lane == row + size, m, 0.0), axis=1, keepdims=True)
    scaled = lax.rsqrt(pivots) * m
    upper = pltpu.roll(jnp.where(lane >= row + size, scaled, 0.0), size, 1)
    return scaled[:, :size], upper[:, :size]


def packed(twice):
    half = twice.shape[0] // 2
    _, lane = iotas(half, twice.shape[1])
    return jnp.where(lane < twice.shape[1] // 2, twice[:half], twice[half:])


def unpacked(pack):
    half, lanes = pack.shape
    _, lane = iotas(half, lanes)
    other = pltpu.roll(pack, lanes // 2, 1)
    first = lane < lanes // 2
    return jnp.concatenate([jnp.where(first, pack, other), jnp.where(first, other, pack)], axis=0)


class Net:
    def __init__(self, send_sems, recv_sems):
        self.send_sems, self.recv_sems = send_sems, recv_sems
        self.sent = []

    def send(self, source, target, **device):
        at = len(self.sent)
        copy = pltpu.make_async_remote_copy(
            src_ref=source,
            dst_ref=target,
            send_sem=self.send_sems.at[at],
            recv_sem=self.recv_sems.at[at],
            device_id=device,
            device_id_type=pl.DeviceIdType.MESH,
        )
        copy.start()
        self.sent.append(copy)
        return copy

    def finish(self):
        for copy in self.sent:
            copy.wait_send()


def body(
    nz, ny,
    g_hbm, b_hbm, p_hbm, n_ref, x_ref, m_ref,
    g_f32, b_own, p_f32, counts, lowest, spread, p_high, p_low,
    b_full, n_full, u_one,
    y_part, y_sib, y_fwd, y_left, y_right,
    az, y_in, z_in, t_out, t_in, i_all, z_all, x_all,
    c_in, sm_own, sm_x, sm_z, sm_y, sm_out,
    g_sems, send_sems, recv_sems,
):
    width, rows_w = b_own.shape
    block = p_f32.shape[0]
    half = width // 2
    quarter = width // 4
    r, c = lax.axis_index("rows"), lax.axis_index("cols")
    x, k = c // CORES, c % CORES
    z, y = r // ny, r % ny
    right = lax.rem(x + 1, CHIPS)
    left = lax.rem(x + CHIPS - 1, CHIPS)
    opposite = lax.rem(x + 2, CHIPS)
    c_sib = x * CORES + 1 - k
    c_right, c_left, c_opp = (chip * CORES + k for chip in (right, left, opposite))
    net = Net(send_sems, recv_sems)

    def chunk(at):
        return pl.ds(pl.multiple_of(at * rows_w, rows_w), rows_w)

    def c_peer(d):
        return lax.rem(c + d, PEERS)

    def z_peer(d):
        return lax.rem(z + d, nz) * ny + y

    def y_peer(d):
        return z * ny + lax.rem(y + d, ny)

    barrier = pltpu.get_barrier_semaphore()
    greeted = [{"rows": z_peer(d)} for d in range(1, nz)]
    greeted += [{"rows": y_peer(d)} for d in range(1, ny)]
    greeted += [{"cols": c_peer(d)} for d in range(1, PEERS)]
    for device in greeted:
        pl.semaphore_signal(barrier, inc=1, device_id=device, device_id_type=pl.DeviceIdType.MESH)

    own_load = pltpu.make_async_copy(b_hbm, b_own, g_sems.at[PEERS])
    p_load = pltpu.make_async_copy(p_hbm, p_f32, g_sems.at[PEERS + 1])
    own_load.start()
    loads = []
    for step, at in enumerate((c, c_sib, c_left, c_right, c_left + 1 - 2 * k, c_right + 1 - 2 * k, c_opp, c_opp + 1 - 2 * k)):
        copy = pltpu.make_async_copy(g_hbm.at[chunk(at)], g_f32.at[chunk(at)], g_sems.at[step])
        copy.start()
        loads.append(copy)
    p_load.start()
    own_load.wait()
    b_own[...] = b_own[...] * (1.0 / SCALE)
    b_full[c] = b_own[...]
    b_gram = exact(b_own[...], doubled(b_own[...]), NT)
    p_load.wait()
    p_high[...], p_low[...] = (v.astype(BF16) for v in parts(p_f32[...])[:2])
    pl.semaphore_wait(barrier, len(greeted))

    work = [iter(())]

    def fill(pieces):
        for _ in range(pieces):
            next(work[0], None)

    def finish(steps):
        for _ in steps:
            pass

    def half_rows(h):
        return (
            pl.ds(h * half, half),
            pl.ds(h * half, quarter),
            pl.ds(h * half + quarter, quarter),
        )

    def gather(full, h, on_block):
        rows, upper, lower = half_rows(h)

        def copy_to(at, rows, target):
            return net.send(full.at[at, rows], full.at[at, rows], cols=target)

        right_upper = copy_to(c, upper, c_right)
        left_lower = copy_to(c, lower, c_left)
        yield
        right_lower = copy_to(c, lower, c_right)
        left_upper = copy_to(c, upper, c_left)
        sib_own = copy_to(c, rows, c_sib)
        yield
        on_block(c, 0)
        right_upper.wait_recv()
        onward_right = copy_to(c_left, upper, c_right)
        sib_left_upper = copy_to(c_left, upper, c_sib)
        left_lower.wait_recv()
        onward_left = copy_to(c_right, lower, c_left)
        sib_right_lower = copy_to(c_right, lower, c_sib)
        yield
        sib_own.wait_recv()
        on_block(c_sib, 1)
        right_lower.wait_recv()
        sib_left_lower = copy_to(c_left, lower, c_sib)
        left_upper.wait_recv()
        sib_right_upper = copy_to(c_right, upper, c_sib)
        on_block(c_left, 2)
        on_block(c_right, 3)
        yield
        sib_left_upper.wait_recv()
        sib_left_lower.wait_recv()
        on_block(c_left + 1 - 2 * k, 4)
        sib_right_lower.wait_recv()
        sib_right_upper.wait_recv()
        on_block(c_right + 1 - 2 * k, 5)
        onward_right.wait_recv()
        sib_opp_upper = copy_to(c_opp, upper, c_sib)
        onward_left.wait_recv()
        sib_opp_lower = copy_to(c_opp, lower, c_sib)
        on_block(c_opp, 6)
        sib_opp_upper.wait_recv()
        sib_opp_lower.wait_recv()
        on_block(c_opp + 1 - 2 * k, 7)

    def scatter(compute, h, part, sib, fwd, from_left, from_right, got):
        rows, upper, lower = half_rows(h)

        def pair(chip, slot):
            mine, theirs = chip * CORES + k, chip * CORES + 1 - k
            part[theirs, rows] = compute(theirs)
            copy = net.send(part.at[theirs, rows], sib.at[slot, rows], cols=c_sib)
            part[mine, rows] = compute(mine)
            return copy

        sib_opp = pair(opposite, 0)
        sib_right = pair(right, 1)
        sib_opp.wait_recv()
        part[c_opp, rows] = part[c_opp, rows] + sib[0, rows]
        fwd_upper = net.send(part.at[c_opp, upper], fwd.at[upper], cols=c_right)
        fwd_lower = net.send(part.at[c_opp, lower], fwd.at[lower], cols=c_left)
        sib_left = pair(left, 2)
        sib_right.wait_recv()
        part[c_right, rows] = part[c_right, rows] + sib[1, rows]
        right_lower = net.send(part.at[c_right, lower], from_left.at[lower], cols=c_right)
        sib_own = pair(x, 3)
        sib_left.wait_recv()
        part[c_left, rows] = part[c_left, rows] + sib[2, rows]
        left_upper = net.send(part.at[c_left, upper], from_right.at[upper], cols=c_left)
        yield
        fwd_upper.wait_recv()
        part[c_right, upper] = part[c_right, upper] + fwd[upper]
        right_upper = net.send(part.at[c_right, upper], from_left.at[upper], cols=c_right)
        fwd_lower.wait_recv()
        part[c_left, lower] = part[c_left, lower] + fwd[lower]
        left_lower = net.send(part.at[c_left, lower], from_right.at[lower], cols=c_left)
        yield
        sib_own.wait_recv()
        total = part[c, rows] + sib[3, rows]
        for copy in (right_lower, left_upper, right_upper, left_lower):
            copy.wait_recv()
        got.append(total + from_left[rows] + from_right[rows])

    share = half // ny

    def p_parts(at):
        lanes = pl.ds(pl.multiple_of(at * block, block), block)
        return p_high[:, lanes], p_low[:, lanes]

    def reduced_and_applied(value, at, h):
        own, yi, zi, to, ti, ia = (b.at[at, h] for b in (az, y_in, z_in, t_out, t_in, i_all))
        za, xa = z_all.at[at], x_all.at[at]
        y_rows = pl.ds(pl.multiple_of(h * half + y * share, share), share)
        own[...] = value
        copies = []
        for d in range(1, ny):
            rows = pl.ds(pl.multiple_of(lax.rem(y + d, ny) * share, share), share)
            copies.append(net.send(own.at[rows], yi.at[d - 1], rows=y_peer(d)))
        yield
        total = own[pl.ds(pl.multiple_of(y * share, share), share)]
        for d in range(1, ny):
            copies[d - 1].wait_recv()
            total = total + yi[d - 1]
        zi[z] = total
        copies = [net.send(zi.at[z], zi.at[z], rows=z_peer(d)) for d in range(1, nz)]
        yield
        for copy in copies:
            copy.wait_recv()
        total = zi[0]
        for i in range(1, nz):
            total = total + zi[i]
        za[y_rows] = total
        copies = []
        for d in range(1, PEERS):
            to[c_peer(d)] = with_parts(total, p_parts(c_peer(d)), NN)
            copies.append(net.send(to.at[c_peer(d)], ti.at[d - 1], cols=c_peer(d)))
        late = [net.send(za.at[y_rows], za.at[y_rows], rows=y_peer(d)) for d in range(1, ny)]
        total = with_parts(total, p_parts(c), NN)
        yield
        for d in range(1, PEERS):
            copies[d - 1].wait_recv()
            total = total + ti[d - 1]
        ia[c] = total
        copies = [net.send(ia.at[c], ia.at[c], cols=c_peer(d)) for d in range(1, PEERS)]
        total = with_parts(total, p_parts(c), NT)
        yield
        for d in range(1, PEERS):
            copies[d - 1].wait_recv()
            source = lax.rem(c + PEERS - d, PEERS)
            total = total + with_parts(ia[source], p_parts(source), NT)
        xa[y_rows] = total
        late += [net.send(xa.at[y_rows], xa.at[y_rows], rows=y_peer(d)) for d in range(1, ny)]
        yield
        for copy in late:
            copy.wait_recv()

    def row_sum(twice, at):
        buffer = c_in.at[at]
        buffer[c] = packed(twice)
        copies = [net.send(buffer.at[c], buffer.at[c], cols=c_peer(d)) for d in range(1, PEERS)]

        def end():
            for copy in copies:
                copy.wait_recv()
            total = buffer[0]
            for i in range(1, PEERS):
                total = total + buffer[i]
            return unpacked(total)

        return end

    def small_sum(value, at):
        piece = width // PEERS
        own, xb, zb, yb, out = (b.at[at] for b in (sm_own, sm_x, sm_z, sm_y, sm_out))
        own[...] = value
        copies = []
        for d in range(1, PEERS):
            rows = pl.ds(pl.multiple_of(c_peer(d) * piece, piece), piece)
            copies.append(net.send(own.at[rows], xb.at[d - 1], cols=c_peer(d)))
        yield
        mine = pl.ds(pl.multiple_of(c * piece, piece), piece)
        total = own[mine]
        for d in range(1, PEERS):
            copies[d - 1].wait_recv()
            total = total + xb[d - 1]
        zb[z] = total
        copies = [net.send(zb.at[z], zb.at[z], rows=z_peer(d)) for d in range(1, nz)]
        yield
        for copy in copies:
            copy.wait_recv()
        total = zb[0]
        for i in range(1, nz):
            total = total + zb[i]
        yb[y] = total
        copies = [net.send(yb.at[y], yb.at[y], rows=y_peer(d)) for d in range(1, ny)]
        yield
        for copy in copies:
            copy.wait_recv()
        total = yb[0]
        for i in range(1, ny):
            total = total + yb[i]
        out[mine] = total
        copies = [net.send(out.at[mine], out.at[mine], cols=c_peer(d)) for d in range(1, PEERS)]
        yield
        for copy in copies:
            copy.wait_recv()

    def through(full, at, before, after_right):
        sums = ([], [])

        def block_of(h):
            rows, _, _ = half_rows(h)

            def on_block(at, step):
                before(at, step, h)
                value = full[at, rows]
                term = with_counts(value, counts[chunk(at)], NN) * spread[at]
                term = term + jnp.sum(value, axis=1, keepdims=True) * lowest[at]
                sums[h].append(term if not sums[h] else sums[h][-1] + term)

            return on_block

        one, two = gather(full, 0, block_of(0)), gather(full, 1, block_of(1))
        next(one)
        next(one)
        next(two)
        next(one)
        next(two)
        finish(one)
        sum_one = reduced_and_applied(sums[0][-1], at, 0)
        next(sum_one)
        finish(two)
        next(sum_one)
        sum_two = reduced_and_applied(sums[1][-1], at, 1)
        next(sum_two)
        fill(4)
        next(sum_two)
        fill(4)
        next(sum_one)
        fill(2)
        next(sum_two)
        fill(4)
        next(sum_one)
        fill(2)
        next(sum_two)
        fill(4)
        next(sum_one)
        fill(2)
        next(sum_two)
        finish(sum_one)

        def forward(h, got):
            value = x_all[at, half_rows(h)[0]]

            def compute(j):
                at_lowest = jnp.sum(value * lowest[j], axis=1, keepdims=True)
                return with_counts(value * spread[j], counts[chunk(j)], NT) + at_lowest

            return scatter(compute, h, *(b.at[at] for b in (y_part, y_sib, y_fwd, y_left, y_right)), got)

        got = []
        one = forward(0, got)
        next(one)
        finish(sum_two)
        finish(work[0])
        work[0] = after_right()
        next(work[0])
        two = forward(1, got)
        next(two)
        next(one)
        fill(2)
        next(two)
        finish(work[0])
        finish(one)
        finish(two)
        return jnp.concatenate(got, axis=0)

    got = {}
    sums = small_sum(b_gram, 0)
    next(sums)

    def load(at, step, h):
        if h == 0:
            loads[step].wait()
            g = g_f32[chunk(at)]
            low = jnp.min(g, axis=0, keepdims=True)
            width_of = jnp.max(g, axis=0, keepdims=True) - low
            one, two = low + 0.25 * width_of, low + 0.75 * width_of
            counts[chunk(at)] = jnp.where(g > two, 2.0, jnp.where(g > one, 1.0, 0.0)).astype(BF16)
            lowest[at] = low
            spread[at] = 0.5 * width_of
        if (h, step) in ((0, 2), (0, 7), (1, 5)):
            next(sums)

    def orthonormal_first():
        finish(sums)
        yield
        done = []
        yield from eliminate([with_identity(sm_out[0])], [False], done)
        got["l0_inv"], got["l0_t"] = factors(done[0])
        yield
        u_one[...] = exact(got["l0_inv"], b_own[...])

    def orthonormal_right():
        l0_inv = got["l0_inv"]
        z_one, x_one = exact(l0_inv, z_all[0]), exact(l0_inv, x_all[0])
        end = row_sum(exact(z_one, doubled(x_one), NT), 0)
        yield
        done = []
        yield from eliminate([with_identity(end())], [False], done)
        got["l1_inv"], got["l1_t"] = factors(done[0])
        yield
        got["x_v"], got["z_v"] = exact(got["l1_inv"], x_one), exact(got["l1_inv"], z_one)
        got["back"] = exact(got["l1_t"], u_one[...])
        got["l1_l0"] = exact(got["l1_inv"], l0_inv)

    work[0] = orthonormal_first()
    y_one = through(b_full, 0, load, orthonormal_right)
    y_v = exact(got["l1_l0"], y_one)
    mapped = y_v - got["back"]
    n_full[c] = mapped
    x_v, z_v, l1_t = got["x_v"], got["z_v"], got["l1_t"]

    def first_target():
        row, lane = iotas(width, width)
        unit = jnp.where(row == lane, 1.0, 0.0)
        got["target_t"] = exact(unit, exact(l1_t, got["l0_t"]), NT)
        yield

    def second_factors():
        z_w, x_w = z_all[1], x_all[1]
        end_h_one = row_sum(exact(x_w, doubled(z_v), NT), 1)
        yield
        h_one = end_h_one()
        h = h_one[:, :width]
        z_j, x_j = z_w - exact(h, z_v), x_w - exact(h, x_v)
        end_e = row_sum(exact(z_j, doubled(x_j), NT), 2)
        normal = exact(l1_t, doubled(l1_t), NT) + h_one
        yield
        done = []
        yield from eliminate([with_identity(h_one), with_identity(normal)], [False, True], done)
        l2_inv, l2_t = factors(done[0])
        s_inv = done[1][:, :width]
        yield
        left_c = exact(l2_inv, end_e()[:, :width])
        c_two = exact(left_c, doubled(l2_inv), NT)
        c_half = c_two[:, :width]
        got["l2_inv"] = l2_inv
        got["back"] = exact(l2_t, y_v) + exact(exact(c_half, l2_inv), mapped)
        cross = exact(c_half, l2_t)
        x_ref[0] = x_v
        x_ref[1] = exact(l2_inv, x_j)
        m_ref[1] = exact(c_half, c_two) - exact(exact(cross, s_inv), doubled(cross), NT)
        m_ref[2] = exact(exact(got["target_t"], s_inv), doubled(cross), NT)
        m_ref[3] = exact(c_half, doubled_lanes(l2_t))
        m_ref[4] = done[1]
        m_ref[5] = doubled_lanes(got["target_t"])

    def doubled_lanes(value):
        row, lane = iotas(width, 2 * width)
        both = jnp.where(jnp.logical_or(lane == row, lane == row + width), 1.0, 0.0)
        return exact(value, both)

    work[0] = first_target()
    y_two = through(n_full, 1, lambda *_: None, second_factors)
    n_two = exact(got["l2_inv"], y_two) - got["back"]
    n_ref[...] = n_two
    finish(small_sum(exact(n_two, doubled(n_two), NT), 1))
    m_ref[0] = sm_out[1]
    net.finish()


def last_block(n_ref, x_ref, m_ref, s_ref, u_ref):
    width = n_ref.shape[0]
    h_two = m_ref[0]
    done = []
    systems = [with_identity(h_two), with_identity(h_two + m_ref[1])]
    for _ in eliminate(systems, [False, True], done):
        pass
    l3_inv, _ = factors(done[0])
    u_ref[...] = exact(l3_inv, n_ref[...])
    b_t = -exact(m_ref[2][:, :width], done[1][:, :width])
    a_t = exact(m_ref[5][:, :width] - exact(b_t, m_ref[3][:, :width]), m_ref[4][:, :width])
    s_ref[...] = SCALE * (exact(a_t, x_ref[0]) + exact(b_t, x_ref[1]))


def solution(mesh, ny=4):
    nrows = mesh.shape["rows"]
    nz = nrows // ny

    def per_device(genotypes, right_sides, inverse_r):
        rows, block = genotypes.shape
        rows_w, width = right_sides.shape
        variants = inverse_r.shape[1]
        half = width // 2
        share = half // ny
        piece = width // PEERS
        v = pltpu.VMEM
        any_space = pl.BlockSpec(memory_space=pl.ANY)
        vmem = pl.BlockSpec(memory_space=pltpu.VMEM)
        messages = 4 * (13 + 10) + 4 * (3 * (ny - 1) + nz - 1 + 2 * (PEERS - 1)) + 3 * (PEERS - 1)
        messages += 2 * (2 * (PEERS - 1) + nz + ny - 2)
        small = pl.pallas_call(
            functools.partial(body, nz, ny),
            out_shape=(
                jax.ShapeDtypeStruct((width, rows_w), F32),
                jax.ShapeDtypeStruct((2, width, block), F32),
                jax.ShapeDtypeStruct((6, width, 2 * width), F32),
            ),
            in_specs=[any_space] * 3,
            out_specs=[vmem] * 3,
            scratch_shapes=[
                v((rows, block), F32), v((width, rows_w), F32), v((block, variants), F32), v((rows, block), BF16),
                v((PEERS, 1, block), F32), v((PEERS, 1, block), F32),
                v((block, variants), BF16), v((block, variants), BF16),
                v((PEERS, width, rows_w), F32), v((PEERS, width, rows_w), F32), v((width, rows_w), F32),
                v((2, PEERS, width, rows_w), F32), v((2, CHIPS, width, rows_w), F32),
                v((2, width, rows_w), F32), v((2, width, rows_w), F32), v((2, width, rows_w), F32),
                v((2, 2, half, block), F32), v((2, 2, max(ny - 1, 1), share, block), F32), v((2, 2, nz, share, block), F32),
                v((2, 2, PEERS, share, block), F32), v((2, 2, PEERS - 1, share, block), F32),
                v((2, 2, PEERS, share, block), F32), v((2, width, block), F32), v((2, width, block), F32),
                v((3, PEERS, half, 2 * width), F32),
                v((2, width, 2 * width), F32), v((2, PEERS - 1, piece, 2 * width), F32),
                v((2, nz, piece, 2 * width), F32), v((2, ny, piece, 2 * width), F32),
                v((2, width, 2 * width), F32),
                pltpu.SemaphoreType.DMA((PEERS + 2,)),
                pltpu.SemaphoreType.DMA((messages,)),
                pltpu.SemaphoreType.DMA((messages,)),
            ],
            compiler_params=pltpu.CompilerParams(
                collective_id=0, has_side_effects=True, vmem_limit_bytes=58 * 1024 * 1024
            ),
        )(genotypes, right_sides.T, inverse_r)
        s_t, u_t = pl.pallas_call(
            last_block,
            out_shape=(
                jax.ShapeDtypeStruct((width, block), F32),
                jax.ShapeDtypeStruct((width, rows_w), F32),
            ),
        )(*small)
        return s_t.T, u_t.T

    in_specs = (P("rows", "cols"), P(("rows", "cols"), None), P("cols", None))
    out_specs = (P("cols", None), P(("rows", "cols"), None))
    return jax.shard_map(
        per_device, mesh=mesh, in_specs=in_specs, out_specs=out_specs, check_vma=False
    )
```

```python
import functools

import jax
import jax.numpy as jnp
from jax import lax
from jax.experimental import pallas as pl
from jax.experimental.pallas import tpu as pltpu
from jax.sharding import PartitionSpec as P

F32 = jnp.float32
BF16 = jnp.bfloat16
NN = (((1,), (0,)), ((), ()))
NT = (((1,), (1,)), ((), ()))
CHIPS = 4
CORES = 2
PEERS = CHIPS * CORES
SCALE = 4096.0


def exact(left, right, dims=NN):
    return lax.dot_general(
        left, right, dims, precision=lax.Precision.HIGHEST, preferred_element_type=F32
    )


def dot(left, right, dims):
    return lax.dot_general(left, right, dims, preferred_element_type=F32)


def parts(value):
    high = value.astype(BF16).astype(F32)
    rest = value - high
    middle = rest.astype(BF16).astype(F32)
    return high, middle, rest - middle


def stacked_parts(value):
    rows = value.shape[0]
    stack = jnp.concatenate(parts(value), axis=0)
    if 3 * rows % 16:
        stack = jnp.concatenate([stack, jnp.zeros((16 - 3 * rows % 16, value.shape[1]), F32)], axis=0)
    return stack.astype(BF16)


def with_counts(value, counts, dims):
    rows = value.shape[0]
    out = dot(stacked_parts(value), counts, dims)
    return out[2 * rows : 3 * rows] + out[rows : 2 * rows] + out[:rows]


def with_parts(value, right, dims):
    rows = value.shape[0]
    stack = stacked_parts(value)
    first = dot(stack, right[0], dims)
    second = dot(stack[: max(2 * rows, 16)], right[1], dims)
    small = first[2 * rows : 3 * rows] + second[rows : 2 * rows]
    return small + (first[rows : 2 * rows] + second[:rows]) + first[:rows]


def beside(value):
    size, lanes = value.shape
    _, lane = iotas(size, lanes)
    return jnp.where(lane < size, value, pltpu.roll(value, size, 1))


def side_by_side(one, two):
    size, lanes = one.shape
    return jnp.where(iotas(size, lanes)[1] < size, one, two)


def doubled(rows):
    return jnp.concatenate([rows, rows], axis=0)


def iotas(rows, lanes):
    row = lax.broadcasted_iota(jnp.int32, (rows, lanes), 0)
    lane = lax.broadcasted_iota(jnp.int32, (rows, lanes), 1)
    return row, lane


def with_identity(twice):
    size = twice.shape[0]
    row, lane = iotas(size, 2 * size)
    return jnp.where(lane < size, jnp.where(lane == row, 1.0, 0.0), twice)


def eliminate(systems, full, done, stride=4):
    size = systems[0].shape[0]
    shape = (size, 2 * size)
    row_at, _ = iotas(*shape)
    systems = list(systems)
    for j in range(0, size, 2):
        for i, m in enumerate(systems):
            first = jnp.broadcast_to(m[:, size + j : size + j + 1], shape)
            second = jnp.broadcast_to(m[:, size + j + 1 : size + j + 2], shape)
            top, bottom = m[j : j + 1, :], m[j + 1 : j + 2, :]
            inverse = 1.0 / first[j : j + 1, :]
            ratio = first[j + 1 : j + 2, :] * inverse
            across = second[j : j + 1, :]
            pivot = 1.0 / (second[j + 1 : j + 2, :] - ratio * across)
            row_two = (bottom - ratio * top) * pivot
            row_one = (top - across * row_two) * inverse
            less = m - first * row_one - second * row_two
            if full[i]:
                systems[i] = jnp.where(row_at == j, row_one, jnp.where(row_at == j + 1, row_two, less))
            else:
                systems[i] = jnp.where(row_at > j + 1, less, m)
        if j // 2 % stride == stride - 1:
            yield
    done.extend(systems)


def factors(m):
    size = m.shape[0]
    row, lane = iotas(size, 2 * size)
    odd = lax.rem(row, 2) == 1
    above = pltpu.roll(m, 1, 0)
    left = jnp.logical_and(odd, lane == row + size - 1)
    under = jnp.sum(jnp.where(left, m, 0.0), axis=1, keepdims=True)
    over = jnp.sum(jnp.where(left, above, jnp.where(jnp.logical_and(lane == 0, jnp.logical_not(odd)), 1.0, 0.0)), axis=1, keepdims=True)
    m = m - (under / over) * above
    pivots = jnp.sum(jnp.where(lane == row + size, m, 0.0), axis=1, keepdims=True)
    scaled = lax.rsqrt(pivots) * m
    upper = pltpu.roll(jnp.where(lane >= row + size, scaled, 0.0), size, 1)
    return beside(scaled), beside(upper)


def packed(twice):
    half = twice.shape[0] // 2
    _, lane = iotas(half, twice.shape[1])
    return jnp.where(lane < twice.shape[1] // 2, twice[:half], twice[half:])


def unpacked(pack):
    half, lanes = pack.shape
    _, lane = iotas(half, lanes)
    other = pltpu.roll(pack, lanes // 2, 1)
    first = lane < lanes // 2
    return jnp.concatenate([jnp.where(first, pack, other), jnp.where(first, other, pack)], axis=0)


class Net:
    def __init__(self, send_sems, recv_sems):
        self.send_sems, self.recv_sems = send_sems, recv_sems
        self.groups, self.arrivals = 0, 0
        self.sent = []

    def group(self, like, together=True):
        sem = self.send_sems.at[self.groups]
        self.groups += 1
        self.sent.append((like, sem))
        arrival = self.next_arrival() if together else None

        def send(source, target, **device):
            copy = pltpu.make_async_remote_copy(
                src_ref=source,
                dst_ref=target,
                send_sem=sem,
                recv_sem=arrival if together else self.next_arrival(),
                device_id=device,
                device_id_type=pl.DeviceIdType.MESH,
            )
            copy.start()
            return copy

        def arrive():
            pltpu.make_async_copy(like, like, arrival).wait()

        return send, arrive

    def next_arrival(self):
        self.arrivals += 1
        return self.recv_sems.at[self.arrivals - 1]

    def finish(self):
        for like, sem in self.sent:
            pltpu.make_async_copy(like, like, sem).wait()


def body(
    nz, ny,
    g_hbm, b_hbm, p_hbm, n_ref, x_ref, m_ref,
    g_f32, b_own, p_f32, counts, lowest, spread, p_high, p_low,
    b_full, n_full, u_one, back,
    y_part, y_sib, y_fwd, y_left, y_right,
    az, z_in, y_in, t_out, t_in, i_all, z_all, x_all,
    c_in, sm_own, sm_x, sm_z, sm_y, sm_out,
    g_sems, send_sems, recv_sems,
):
    width, rows_w = b_own.shape
    block = p_f32.shape[0]
    half = width // 2
    r, c = lax.axis_index("rows"), lax.axis_index("cols")
    x, k = c // CORES, c % CORES
    z, y = r // ny, r % ny
    right = lax.rem(x + 1, CHIPS)
    left = lax.rem(x + CHIPS - 1, CHIPS)
    opposite = lax.rem(x + 2, CHIPS)
    c_sib = x * CORES + 1 - k
    c_right, c_left, c_opp = (chip * CORES + k for chip in (right, left, opposite))
    net = Net(send_sems, recv_sems)

    def chunk(at):
        return pl.ds(pl.multiple_of(at * rows_w, rows_w), rows_w)

    def c_peer(d):
        return lax.rem(c + d, PEERS)

    def z_peer(d):
        return lax.rem(z + d, nz) * ny + y

    def y_peer(d):
        return z * ny + lax.rem(y + d, ny)

    barrier = pltpu.get_barrier_semaphore()
    greeted = [{"rows": z_peer(d)} for d in range(1, nz)]
    greeted += [{"rows": y_peer(d)} for d in range(1, ny)]
    greeted += [{"cols": c_peer(d)} for d in range(1, PEERS)]
    for device in greeted:
        pl.semaphore_signal(barrier, inc=1, device_id=device, device_id_type=pl.DeviceIdType.MESH)

    own_load = pltpu.make_async_copy(b_hbm, b_own, g_sems.at[PEERS])
    p_load = pltpu.make_async_copy(p_hbm, p_f32, g_sems.at[PEERS + 1])
    own_load.start()
    loads = []
    for step, at in enumerate((c, c_sib, c_left, c_right, c_left + 1 - 2 * k, c_right + 1 - 2 * k, c_opp, c_opp + 1 - 2 * k)):
        copy = pltpu.make_async_copy(g_hbm.at[chunk(at)], g_f32.at[chunk(at)], g_sems.at[step])
        copy.start()
        loads.append(copy)
    p_load.start()
    own_load.wait()
    b_own[...] = b_own[...] * (1.0 / SCALE)
    b_full[c] = b_own[...]
    b_gram = exact(b_own[...], doubled(b_own[...]), NT)
    p_load.wait()
    p_high[...], p_low[...] = (v.astype(BF16) for v in parts(p_f32[...])[:2])
    pl.semaphore_wait(barrier, len(greeted))

    work = [iter(())]
    got = {}

    def fill(pieces):
        for _ in range(pieces):
            next(work[0], None)

    def finish(steps):
        for _ in steps:
            pass

    upper, lower = pl.ds(0, half), pl.ds(half, half)
    tiles = rows_w // 128
    cut = (tiles + 1) // 2 * 128
    pieces = (pl.ds(0, cut), pl.ds(cut, rows_w - cut)) if tiles > 1 else (pl.ds(0, rows_w),)
    whole = pl.ds(0, rows_w)

    def samples(at, lanes):
        return pl.ds(pl.multiple_of(at * rows_w + lanes.start, 128), lanes.size)

    def gather(full, lanes, on_block):
        send, _ = net.group(full.at[pl.ds(0, PEERS - 1), :, lanes], together=False)

        def copy_to(at, rows, target):
            return send(full.at[at, rows, lanes], full.at[at, rows, lanes], cols=target)

        right_upper = copy_to(c, upper, c_right)
        left_lower = copy_to(c, lower, c_left)
        right_lower = copy_to(c, lower, c_right)
        left_upper = copy_to(c, upper, c_left)
        sib_own = send(full.at[c, :, lanes], full.at[c, :, lanes], cols=c_sib)
        yield
        on_block(c, 0)
        right_upper.wait_recv()
        onward_right = copy_to(c_left, upper, c_right)
        sib_left_upper = copy_to(c_left, upper, c_sib)
        left_lower.wait_recv()
        onward_left = copy_to(c_right, lower, c_left)
        sib_right_lower = copy_to(c_right, lower, c_sib)
        yield
        sib_own.wait_recv()
        on_block(c_sib, 1)
        right_lower.wait_recv()
        sib_left_lower = copy_to(c_left, lower, c_sib)
        left_upper.wait_recv()
        sib_right_upper = copy_to(c_right, upper, c_sib)
        on_block(c_left, 2)
        on_block(c_right, 3)
        sib_left_upper.wait_recv()
        sib_left_lower.wait_recv()
        on_block(c_left + 1 - 2 * k, 4)
        sib_right_lower.wait_recv()
        sib_right_upper.wait_recv()
        on_block(c_right + 1 - 2 * k, 5)
        onward_right.wait_recv()
        sib_opp_upper = copy_to(c_opp, upper, c_sib)
        onward_left.wait_recv()
        sib_opp_lower = copy_to(c_opp, lower, c_sib)
        on_block(c_opp, 6)
        sib_opp_upper.wait_recv()
        sib_opp_lower.wait_recv()
        on_block(c_opp + 1 - 2 * k, 7)

    def scatter(compute, lanes, part, sib, fwd, from_left, from_right, got):
        send, _ = net.group(part.at[pl.ds(0, PEERS - 1), :, lanes], together=False)

        def pair(chip, slot):
            mine, theirs = chip * CORES + k, chip * CORES + 1 - k
            part[theirs, :, lanes] = compute(theirs)
            copy = send(part.at[theirs, :, lanes], sib.at[slot, :, lanes], cols=c_sib)
            part[mine, :, lanes] = compute(mine)
            return copy

        sib_opp = pair(opposite, 0)
        sib_right = pair(right, 1)
        sib_opp.wait_recv()
        part[c_opp, :, lanes] = part[c_opp, :, lanes] + sib[0, :, lanes]
        fwd_upper = send(part.at[c_opp, upper, lanes], fwd.at[upper, lanes], cols=c_right)
        fwd_lower = send(part.at[c_opp, lower, lanes], fwd.at[lower, lanes], cols=c_left)
        yield
        sib_left = pair(left, 2)
        sib_right.wait_recv()
        part[c_right, :, lanes] = part[c_right, :, lanes] + sib[1, :, lanes]
        right_lower = send(part.at[c_right, lower, lanes], from_left.at[lower, lanes], cols=c_right)
        sib_own = pair(x, 3)
        sib_left.wait_recv()
        part[c_left, :, lanes] = part[c_left, :, lanes] + sib[2, :, lanes]
        left_upper = send(part.at[c_left, upper, lanes], from_right.at[upper, lanes], cols=c_left)
        yield
        fwd_upper.wait_recv()
        part[c_right, upper, lanes] = part[c_right, upper, lanes] + fwd[upper, lanes]
        right_upper = send(part.at[c_right, upper, lanes], from_left.at[upper, lanes], cols=c_right)
        fwd_lower.wait_recv()
        part[c_left, lower, lanes] = part[c_left, lower, lanes] + fwd[lower, lanes]
        left_lower = send(part.at[c_left, lower, lanes], from_right.at[lower, lanes], cols=c_left)
        yield
        sib_own.wait_recv()
        total = part[c, :, lanes] + sib[3, :, lanes]
        for copy in (right_lower, left_upper, right_upper, left_lower):
            copy.wait_recv()
        got.append(total + from_left[:, lanes] + from_right[:, lanes])

    share = width // nz
    z_rows = pl.ds(pl.multiple_of(z * share, share), share)

    def p_parts(at):
        lanes = pl.ds(pl.multiple_of(at * block, block), block)
        return p_high[:, lanes], p_low[:, lanes]

    def reduced_and_applied(value, at):
        lanes = pl.ds(0, value.shape[1])
        own, zi, yi, to, ti, ia, za, xa = (b.at[at] for b in (az, z_in, y_in, t_out, t_in, i_all, z_all, x_all))
        own[:, lanes] = value
        send, arrive = net.group(zi.at[:, :, lanes])
        for d in range(1, nz):
            rows = pl.ds(pl.multiple_of(lax.rem(z + d, nz) * share, share), share)
            send(own.at[rows, lanes], zi.at[d - 1, :, lanes], rows=z_peer(d))
        yield
        total = own[z_rows, lanes]
        arrive()
        for d in range(1, nz):
            total = total + zi[d - 1, :, lanes]
        yi[y, :, lanes] = total
        if ny > 1:
            send, arrive = net.group(yi.at[pl.ds(0, ny - 1), :, lanes])
            for d in range(1, ny):
                send(yi.at[y, :, lanes], yi.at[y, :, lanes], rows=y_peer(d))
        yield
        if ny > 1:
            arrive()
        total = yi[0, :, lanes]
        for i in range(1, ny):
            total = total + yi[i, :, lanes]
        za[z_rows, lanes] = total
        total = total[:, :block]
        send, arrive = net.group(ti)
        for d in range(1, PEERS):
            to[c_peer(d)] = with_parts(total, p_parts(c_peer(d)), NN)
            send(to.at[c_peer(d)], ti.at[d - 1], cols=c_peer(d))
        send, got["summed"] = net.group(za.at[pl.ds(0, (nz - 1) * share), lanes])
        for d in range(1, nz):
            send(za.at[z_rows, lanes], za.at[z_rows, lanes], rows=z_peer(d))
        total = with_parts(total, p_parts(c), NN)
        yield
        arrive()
        for d in range(1, PEERS):
            total = total + ti[d - 1]
        ia[c] = total
        send, arrive = net.group(ia.at[pl.ds(0, PEERS - 1)])
        for d in range(1, PEERS):
            send(ia.at[c], ia.at[c], cols=c_peer(d))
        total = with_parts(total, p_parts(c), NT)
        yield
        arrive()
        for d in range(1, PEERS):
            source = lax.rem(c + PEERS - d, PEERS)
            total = total + with_parts(ia[source], p_parts(source), NT)
        xa[z_rows] = total
        send, arrive = net.group(xa.at[pl.ds(0, (nz - 1) * share)])
        for d in range(1, nz):
            send(xa.at[z_rows], xa.at[z_rows], rows=z_peer(d))
        yield
        arrive()

    def row_sum(twice, at):
        buffer = c_in.at[at]
        buffer[c] = packed(twice)
        send, arrive = net.group(buffer.at[pl.ds(0, PEERS - 1)])
        for d in range(1, PEERS):
            send(buffer.at[c], buffer.at[c], cols=c_peer(d))

        def end():
            arrive()
            total = buffer[0]
            for i in range(1, PEERS):
                total = total + buffer[i]
            return unpacked(total)

        return end

    def small_sum(value):
        piece = width // PEERS
        mine = pl.ds(pl.multiple_of(c * piece, piece), piece)
        sm_own[...] = value
        send, arrive = net.group(sm_x)
        for d in range(1, PEERS):
            rows = pl.ds(pl.multiple_of(c_peer(d) * piece, piece), piece)
            send(sm_own.at[rows], sm_x.at[d - 1], cols=c_peer(d))
        yield
        total = sm_own[mine]
        arrive()
        for d in range(1, PEERS):
            total = total + sm_x[d - 1]
        sm_z[z] = total
        send, arrive = net.group(sm_z.at[pl.ds(0, nz - 1)])
        for d in range(1, nz):
            send(sm_z.at[z], sm_z.at[z], rows=z_peer(d))
        yield
        arrive()
        total = sm_z[0]
        for i in range(1, nz):
            total = total + sm_z[i]
        sm_y[y] = total
        if ny > 1:
            send, arrive = net.group(sm_y.at[pl.ds(0, ny - 1)])
            for d in range(1, ny):
                send(sm_y.at[y], sm_y.at[y], rows=y_peer(d))
        yield
        if ny > 1:
            arrive()
        total = sm_y[0]
        for i in range(1, ny):
            total = total + sm_y[i]
        sm_out[mine] = total
        send, arrive = net.group(sm_out.at[pl.ds(0, width - piece)])
        for d in range(1, PEERS):
            send(sm_out.at[mine], sm_out.at[mine], cols=c_peer(d))
        yield
        arrive()

    def backward(full, lanes, sums, before=lambda at, step: None):
        def on_block(at, step):
            before(at, step)
            value = full[at, :, lanes]
            term = with_counts(value, counts[samples(at, lanes)], NN) * spread[at]
            term = term + jnp.sum(value, axis=1, keepdims=True) * lowest[at]
            sums.append(term if not sums else sums[-1] + term)

        return gather(full, lanes, on_block)

    def forward(value, lanes, at, got):
        def compute(j):
            at_lowest = jnp.sum(value * lowest[j], axis=1, keepdims=True)
            return with_counts(value * spread[j], counts[samples(j, lanes)], NT) + at_lowest

        return scatter(compute, lanes, *(b.at[at] for b in (y_part, y_sib, y_fwd, y_left, y_right)), got)

    def in_shares(value, at):
        for step, _ in enumerate(reduced_and_applied(value, at)):
            if step >= 3:
                fill(6)
        finish(work[0])
        return z_all[at], x_all[at]

    end_gram = row_sum(b_gram, 0)

    def load(at, step):
        loads[step].wait()
        g = g_f32[chunk(at)]
        low = jnp.min(g, axis=0, keepdims=True)
        width_of = jnp.max(g, axis=0, keepdims=True) - low
        one, two = low + 0.25 * width_of, low + 0.75 * width_of
        counts[chunk(at)] = jnp.where(g > two, 2.0, jnp.where(g > one, 1.0, 0.0)).astype(BF16)
        lowest[at] = low
        spread[at] = 0.5 * width_of

    def orthonormal_first():
        got["summed"]()
        done = []
        yield from eliminate([with_identity(z_all[0, :, block:])], [False], done)
        got["two_l0_inv"], two_l0_t = factors(done[0])
        got["l0_inv"], got["l0_t"] = got["two_l0_inv"][:, :width], two_l0_t[:, :width]
        yield
        u_one[...] = exact(got["l0_inv"], b_own[...])

    totals = []
    finish(backward(b_full, whole, totals, load))
    work[0] = orthonormal_first()
    z_raw, x_raw = in_shares(jnp.concatenate([totals[-1], end_gram()], axis=1), 0)
    z_raw = z_raw[:, :block]

    def orthonormal_right():
        l0_inv = got["l0_inv"]
        z_one, x_one = exact(l0_inv, z_raw), exact(l0_inv, x_raw)
        end = row_sum(exact(z_one, doubled(x_one), NT), 1)
        yield
        done = []
        yield from eliminate([with_identity(end())], [False], done)
        two_l1_inv, got["two_l1_t"] = factors(done[0])
        got["l1_inv"], got["l1_t"] = two_l1_inv[:, :width], got["two_l1_t"][:, :width]
        got["left"] = side_by_side(exact(got["l1_inv"], got["two_l0_inv"]), -got["two_l1_t"])
        got["one"] = x_one, z_one

    work[0] = orthonormal_right()
    halves = []
    scatters = [forward(x_raw, lanes, 0, halves) for lanes in pieces]
    first, second = scatters[0], scatters[-1]
    fill(1)
    next(first)
    next(first)
    next(second)
    fill(3)
    next(first)
    next(second)
    fill(4)
    next(second)
    finish(work[0])
    l1_t = got["l1_t"]
    totals, gathers = [], []
    for lanes, steps in zip(pieces, scatters):
        finish(steps)
        n_full[c, :, lanes] = exact(got["left"], jnp.concatenate([halves[-1], u_one[:, lanes]], axis=0))
        gathers.append(backward(n_full, lanes, totals))
        next(gathers[-1])
    x_v, z_v = (exact(got["l1_inv"], v) for v in got["one"])
    for steps in gathers:
        next(steps)
    for steps in gathers:
        finish(steps)

    def first_target():
        got["summed"]()
        row, lane = iotas(width, width)
        unit = jnp.where(row == lane, 1.0, 0.0)
        got["target_t"] = exact(unit, exact(l1_t, got["l0_t"]), NT)
        yield

    def second_factors():
        end_h_one = row_sum(exact(x_w, doubled(z_v), NT), 2)
        yield
        h_one = end_h_one()
        h = h_one[:, :width]
        z_j, x_j = z_w - exact(h, z_v), x_w - exact(h, x_v)
        end_e = row_sum(exact(z_j, doubled(x_j), NT), 3)
        normal = exact(l1_t, doubled(l1_t), NT) + h_one
        yield
        done = []
        yield from eliminate([with_identity(h_one), with_identity(normal)], [False, True], done)
        two_l2_inv, two_l2_t = factors(done[0])
        l2_inv, l2_t = two_l2_inv[:, :width], two_l2_t[:, :width]
        s_inv = done[1][:, :width]
        yield
        left_c = exact(l2_inv, end_e()[:, :width])
        c_two = exact(left_c, doubled(l2_inv), NT)
        c_half = c_two[:, :width]
        got["l2_inv"] = l2_inv
        back_left = side_by_side(two_l2_t + exact(c_half, two_l2_inv), exact(l2_t, got["two_l1_t"]))
        back[...] = exact(back_left, jnp.concatenate([n_full[c], u_one[...]], axis=0))
        got["second"] = x_j, l2_inv, two_l2_t, s_inv, done[1], c_half, c_two

    def rest():
        x_j, l2_inv, two_l2_t, s_inv, s_full, c_half, c_two = got["second"]
        two_cross = exact(c_half, two_l2_t)
        cross = two_cross[:, :width]
        x_ref[0] = x_v
        x_ref[1] = exact(l2_inv, x_j)
        m_ref[1] = exact(c_half, c_two) - exact(exact(cross, s_inv), doubled(cross), NT)
        yield
        m_ref[2] = exact(exact(got["target_t"], s_inv), doubled(cross), NT)
        m_ref[3] = two_cross
        m_ref[4] = s_full
        m_ref[5] = doubled_lanes(got["target_t"])

    def doubled_lanes(value):
        row, lane = iotas(width, 2 * width)
        both = jnp.where(jnp.logical_or(lane == row, lane == row + width), 1.0, 0.0)
        return exact(value, both)

    work[0] = first_target()
    z_w, x_w = in_shares(totals[-1], 1)
    z_w = z_w[:, :block]
    work[0] = second_factors()
    halves = []
    scatters = [forward(x_w, lanes, 1, halves) for lanes in pieces]
    first, second = scatters[0], scatters[-1]
    fill(1)
    next(first)
    next(first)
    next(second)
    fill(2)
    next(first)
    next(second)
    fill(2)
    next(second)
    finish(work[0])
    n_gram = None
    for lanes, steps in zip(pieces, scatters):
        finish(steps)
        n_two = exact(got["l2_inv"], halves[-1]) - back[:, lanes]
        n_ref[:, lanes] = n_two
        term = exact(n_two, doubled(n_two), NT)
        n_gram = term if n_gram is None else n_gram + term
    work[0] = rest()
    for _ in small_sum(n_gram):
        fill(1)
    finish(work[0])
    m_ref[0] = sm_out[...]
    net.finish()


def last_block(n_ref, x_ref, m_ref, s_ref, u_ref):
    width = n_ref.shape[0]
    h_two = m_ref[0]
    done = []
    systems = [with_identity(h_two), with_identity(h_two + m_ref[1])]
    for _ in eliminate(systems, [False, True], done):
        pass
    l3_inv, _ = factors(done[0])
    u_ref[...] = exact(l3_inv[:, :width], n_ref[...])
    b_t = -exact(m_ref[2][:, :width], done[1][:, :width])
    a_t = exact(m_ref[5][:, :width] - exact(b_t, m_ref[3][:, :width]), m_ref[4][:, :width])
    s_ref[...] = SCALE * (exact(a_t, x_ref[0]) + exact(b_t, x_ref[1]))


def solution(mesh, ny=4):
    nrows = mesh.shape["rows"]
    nz = nrows // ny

    def per_device(genotypes, right_sides, inverse_r):
        rows, block = genotypes.shape
        rows_w, width = right_sides.shape
        variants = inverse_r.shape[1]
        half = width // 2
        share = width // nz
        piece = width // PEERS
        v = pltpu.VMEM
        any_space = pl.BlockSpec(memory_space=pl.ANY)
        vmem = pl.BlockSpec(memory_space=pltpu.VMEM)
        beside = block + 2 * width
        together = 2 * 6 + 4 + 4
        groups = together + 3 + 4
        arrivals = together + 3 * 13 + 4 * 10
        small = pl.pallas_call(
            functools.partial(body, nz, ny),
            out_shape=(
                jax.ShapeDtypeStruct((width, rows_w), F32),
                jax.ShapeDtypeStruct((2, width, block), F32),
                jax.ShapeDtypeStruct((6, width, 2 * width), F32),
            ),
            in_specs=[any_space] * 3,
            out_specs=[vmem] * 3,
            scratch_shapes=[
                v((rows, block), F32), v((width, rows_w), F32), v((block, variants), F32), v((rows, block), BF16),
                v((PEERS, 1, block), F32), v((PEERS, 1, block), F32),
                v((block, variants), BF16), v((block, variants), BF16),
                v((PEERS, width, rows_w), F32), v((PEERS, width, rows_w), F32),
                v((width, rows_w), F32), v((width, rows_w), F32),
                v((2, PEERS, width, rows_w), F32), v((2, CHIPS, width, rows_w), F32),
                v((2, width, rows_w), F32), v((2, width, rows_w), F32), v((2, width, rows_w), F32),
                v((2, width, beside), F32), v((2, nz - 1, share, beside), F32), v((2, ny, share, beside), F32),
                v((2, PEERS, share, block), F32), v((2, PEERS - 1, share, block), F32),
                v((2, PEERS, share, block), F32), v((2, width, beside), F32), v((2, width, block), F32),
                v((4, PEERS, half, 2 * width), F32),
                v((width, 2 * width), F32), v((PEERS - 1, piece, 2 * width), F32),
                v((nz, piece, 2 * width), F32), v((ny, piece, 2 * width), F32), v((width, 2 * width), F32),
                pltpu.SemaphoreType.DMA((PEERS + 2,)),
                pltpu.SemaphoreType.DMA((groups,)),
                pltpu.SemaphoreType.DMA((arrivals,)),
            ],
            compiler_params=pltpu.CompilerParams(
                collective_id=0, has_side_effects=True, vmem_limit_bytes=58 * 1024 * 1024
            ),
        )(genotypes, right_sides.T, inverse_r)
        s_t, u_t = pl.pallas_call(
            last_block,
            out_shape=(
                jax.ShapeDtypeStruct((width, block), F32),
                jax.ShapeDtypeStruct((width, rows_w), F32),
            ),
        )(*small)
        return s_t.T, u_t.T

    in_specs = (P("rows", "cols"), P(("rows", "cols"), None), P("cols", None))
    out_specs = (P("cols", None), P(("rows", "cols"), None))
    return jax.shard_map(
        per_device, mesh=mesh, in_specs=in_specs, out_specs=out_specs, check_vma=False
    )
```

```python
import functools

import jax
import jax.numpy as jnp
from jax import lax
from jax.experimental import pallas as pl
from jax.experimental.pallas import tpu as pltpu
from jax.sharding import PartitionSpec as P

F32 = jnp.float32
BF16 = jnp.bfloat16
NN = (((1,), (0,)), ((), ()))
NT = (((1,), (1,)), ((), ()))
CHIPS = 4
CORES = 2
PEERS = CHIPS * CORES
SCALE = 4096.0


def exact(left, right, dims=NN):
    return lax.dot_general(
        left, right, dims, precision=lax.Precision.HIGHEST, preferred_element_type=F32
    )


def dot(left, right, dims):
    return lax.dot_general(left, right, dims, preferred_element_type=F32)


def parts(value):
    high = value.astype(BF16).astype(F32)
    rest = value - high
    middle = rest.astype(BF16).astype(F32)
    return high, middle, rest - middle


def stacked_parts(value):
    rows = value.shape[0]
    stack = jnp.concatenate(parts(value), axis=0)
    if 3 * rows % 16:
        stack = jnp.concatenate([stack, jnp.zeros((16 - 3 * rows % 16, value.shape[1]), F32)], axis=0)
    return stack.astype(BF16)


def with_counts(value, counts, dims):
    rows = value.shape[0]
    out = dot(stacked_parts(value), counts, dims)
    return out[2 * rows : 3 * rows] + out[rows : 2 * rows] + out[:rows]


def with_parts(value, right, dims):
    rows = value.shape[0]
    stack = stacked_parts(value)
    first = dot(stack, right[0], dims)
    second = dot(stack[: max(2 * rows, 16)], right[1], dims)
    small = first[2 * rows : 3 * rows] + second[rows : 2 * rows]
    return small + (first[rows : 2 * rows] + second[:rows]) + first[:rows]


def beside(value):
    size, lanes = value.shape
    _, lane = iotas(size, lanes)
    return jnp.where(lane < size, value, pltpu.roll(value, size, 1))


def side_by_side(one, two):
    size, lanes = one.shape
    return jnp.where(iotas(size, lanes)[1] < size, one, two)


def doubled(rows):
    return jnp.concatenate([rows, rows], axis=0)


def iotas(rows, lanes):
    row = lax.broadcasted_iota(jnp.int32, (rows, lanes), 0)
    lane = lax.broadcasted_iota(jnp.int32, (rows, lanes), 1)
    return row, lane


def with_identity(twice):
    size = twice.shape[0]
    row, lane = iotas(size, 2 * size)
    return jnp.where(lane < size, jnp.where(lane == row, 1.0, 0.0), twice)


def eliminate(systems, full, done, stride=4):
    size = systems[0].shape[0]
    shape = (size, 2 * size)
    row_at, _ = iotas(*shape)
    systems = list(systems)
    for j in range(0, size, 2):
        for i, m in enumerate(systems):
            first = jnp.broadcast_to(m[:, size + j : size + j + 1], shape)
            second = jnp.broadcast_to(m[:, size + j + 1 : size + j + 2], shape)
            top, bottom = m[j : j + 1, :], m[j + 1 : j + 2, :]
            inverse = 1.0 / first[j : j + 1, :]
            ratio = first[j + 1 : j + 2, :] * inverse
            across = second[j : j + 1, :]
            pivot = 1.0 / (second[j + 1 : j + 2, :] - ratio * across)
            row_two = (bottom - ratio * top) * pivot
            row_one = (top - across * row_two) * inverse
            less = m - first * row_one - second * row_two
            if full[i]:
                systems[i] = jnp.where(row_at == j, row_one, jnp.where(row_at == j + 1, row_two, less))
            else:
                systems[i] = jnp.where(row_at > j + 1, less, m)
        if j // 2 % stride == stride - 1:
            yield
    done.extend(systems)


def factors(m):
    size = m.shape[0]
    row, lane = iotas(size, 2 * size)
    odd = lax.rem(row, 2) == 1
    above = pltpu.roll(m, 1, 0)
    left = jnp.logical_and(odd, lane == row + size - 1)
    under = jnp.sum(jnp.where(left, m, 0.0), axis=1, keepdims=True)
    over = jnp.sum(jnp.where(left, above, jnp.where(jnp.logical_and(lane == 0, jnp.logical_not(odd)), 1.0, 0.0)), axis=1, keepdims=True)
    m = m - (under / over) * above
    pivots = jnp.sum(jnp.where(lane == row + size, m, 0.0), axis=1, keepdims=True)
    scaled = lax.rsqrt(pivots) * m
    upper = pltpu.roll(jnp.where(lane >= row + size, scaled, 0.0), size, 1)
    return beside(scaled), beside(upper)


def packed(twice):
    half = twice.shape[0] // 2
    _, lane = iotas(half, twice.shape[1])
    return jnp.where(lane < twice.shape[1] // 2, twice[:half], twice[half:])


def unpacked(pack):
    half, lanes = pack.shape
    _, lane = iotas(half, lanes)
    other = pltpu.roll(pack, lanes // 2, 1)
    first = lane < lanes // 2
    return jnp.concatenate([jnp.where(first, pack, other), jnp.where(first, other, pack)], axis=0)


class Net:
    def __init__(self, send_sems, recv_sems):
        self.send_sems, self.recv_sems = send_sems, recv_sems
        self.groups, self.arrivals = 0, 0
        self.sent = []

    def group(self, like, together=True):
        sem = self.send_sems.at[self.groups]
        self.groups += 1
        self.sent.append((like, sem))
        arrival = self.next_arrival() if together else None

        def send(source, target, **device):
            copy = pltpu.make_async_remote_copy(
                src_ref=source,
                dst_ref=target,
                send_sem=sem,
                recv_sem=arrival if together else self.next_arrival(),
                device_id=device,
                device_id_type=pl.DeviceIdType.MESH,
            )
            copy.start()
            return copy

        def arrive():
            pltpu.make_async_copy(like, like, arrival).wait()

        return send, arrive

    def next_arrival(self):
        self.arrivals += 1
        return self.recv_sems.at[self.arrivals - 1]

    def finish(self):
        for like, sem in self.sent:
            pltpu.make_async_copy(like, like, sem).wait()


def body(
    nz, ny,
    g_hbm, b_hbm, p_hbm, n_ref, x_ref, m_ref,
    g_f32, b_own, p_f32, counts, lowest, spread, p_high, p_low,
    b_full, n_full, u_one, back,
    y_part, y_sib, y_fwd, y_left, y_right,
    az, z_in, y_in, t_out, t_in, i_all, z_all, x_all,
    c_in, sm_own, sm_x, sm_z, sm_y, sm_out,
    g_sems, send_sems, recv_sems,
):
    width, rows_w = b_own.shape
    block = p_f32.shape[0]
    half = width // 2
    r, c = lax.axis_index("rows"), lax.axis_index("cols")
    x, k = c // CORES, c % CORES
    z, y = r // ny, r % ny
    right = lax.rem(x + 1, CHIPS)
    left = lax.rem(x + CHIPS - 1, CHIPS)
    opposite = lax.rem(x + 2, CHIPS)
    c_sib = x * CORES + 1 - k
    c_right, c_left, c_opp = (chip * CORES + k for chip in (right, left, opposite))
    net = Net(send_sems, recv_sems)

    def chunk(at):
        return pl.ds(pl.multiple_of(at * rows_w, rows_w), rows_w)

    def c_peer(d):
        return lax.rem(c + d, PEERS)

    def z_peer(d):
        return lax.rem(z + d, nz) * ny + y

    def y_peer(d):
        return z * ny + lax.rem(y + d, ny)

    barrier = pltpu.get_barrier_semaphore()
    greeted = [{"rows": z_peer(d)} for d in range(1, nz)]
    greeted += [{"rows": y_peer(d)} for d in range(1, ny)]
    greeted += [{"cols": c_peer(d)} for d in range(1, PEERS)]
    for device in greeted:
        pl.semaphore_signal(barrier, inc=1, device_id=device, device_id_type=pl.DeviceIdType.MESH)

    own_load = pltpu.make_async_copy(b_hbm, b_own, g_sems.at[PEERS])
    p_load = pltpu.make_async_copy(p_hbm, p_f32, g_sems.at[PEERS + 1])
    own_load.start()
    loads = []
    order = (c, c_sib, c_left, c_right, c_left + 1 - 2 * k, c_right + 1 - 2 * k, c_opp, c_opp + 1 - 2 * k)
    for step, at in enumerate(order):
        copy = pltpu.make_async_copy(g_hbm.at[chunk(at)], g_f32.at[chunk(at)], g_sems.at[step])
        copy.start()
        loads.append(copy)
    p_load.start()
    own_load.wait()
    b_own[...] = b_own[...] * (1.0 / SCALE)
    b_full[c] = b_own[...]
    b_gram = exact(b_own[...], doubled(b_own[...]), NT)
    p_load.wait()
    p_high[...], p_low[...] = (v.astype(BF16) for v in parts(p_f32[...])[:2])
    pl.semaphore_wait(barrier, len(greeted))

    work = [iter(())]
    got = {}

    def fill(pieces):
        for _ in range(pieces):
            next(work[0], None)

    def finish(steps):
        for _ in steps:
            pass

    upper, lower = pl.ds(0, half), pl.ds(half, half)
    tiles = rows_w // 128
    cut = (tiles + 1) // 2 * 128
    pieces = (pl.ds(0, cut), pl.ds(cut, rows_w - cut)) if tiles > 1 else (pl.ds(0, rows_w),)
    whole = pl.ds(0, rows_w)

    def samples(at, lanes):
        return pl.ds(pl.multiple_of(at * rows_w + lanes.start, 128), lanes.size)

    def gather(full, lanes, on_block):
        send, _ = net.group(full.at[pl.ds(0, PEERS - 1), :, lanes], together=False)

        def copy_to(at, rows, target):
            return send(full.at[at, rows, lanes], full.at[at, rows, lanes], cols=target)

        right_upper = copy_to(c, upper, c_right)
        left_lower = copy_to(c, lower, c_left)
        right_lower = copy_to(c, lower, c_right)
        left_upper = copy_to(c, upper, c_left)
        sib_own = send(full.at[c, :, lanes], full.at[c, :, lanes], cols=c_sib)
        yield
        on_block(c, 0)
        right_upper.wait_recv()
        onward_right = copy_to(c_left, upper, c_right)
        sib_left_upper = copy_to(c_left, upper, c_sib)
        left_lower.wait_recv()
        onward_left = copy_to(c_right, lower, c_left)
        sib_right_lower = copy_to(c_right, lower, c_sib)
        yield
        sib_own.wait_recv()
        on_block(c_sib, 1)
        right_lower.wait_recv()
        sib_left_lower = copy_to(c_left, lower, c_sib)
        left_upper.wait_recv()
        sib_right_upper = copy_to(c_right, upper, c_sib)
        on_block(c_left, 2)
        on_block(c_right, 3)
        sib_left_upper.wait_recv()
        sib_left_lower.wait_recv()
        on_block(c_left + 1 - 2 * k, 4)
        sib_right_lower.wait_recv()
        sib_right_upper.wait_recv()
        on_block(c_right + 1 - 2 * k, 5)
        onward_right.wait_recv()
        sib_opp_upper = copy_to(c_opp, upper, c_sib)
        onward_left.wait_recv()
        sib_opp_lower = copy_to(c_opp, lower, c_sib)
        on_block(c_opp, 6)
        sib_opp_upper.wait_recv()
        sib_opp_lower.wait_recv()
        on_block(c_opp + 1 - 2 * k, 7)

    def scatter(compute, lanes, part, sib, fwd, from_left, from_right, got):
        send, _ = net.group(part.at[pl.ds(0, PEERS - 1), :, lanes], together=False)

        def pair(chip, slot):
            mine, theirs = chip * CORES + k, chip * CORES + 1 - k
            part[theirs, :, lanes] = compute(theirs)
            copy = send(part.at[theirs, :, lanes], sib.at[slot, :, lanes], cols=c_sib)
            part[mine, :, lanes] = compute(mine)
            return copy

        sib_opp = pair(opposite, 0)
        sib_right = pair(right, 1)
        sib_opp.wait_recv()
        part[c_opp, :, lanes] = part[c_opp, :, lanes] + sib[0, :, lanes]
        fwd_upper = send(part.at[c_opp, upper, lanes], fwd.at[upper, lanes], cols=c_right)
        fwd_lower = send(part.at[c_opp, lower, lanes], fwd.at[lower, lanes], cols=c_left)
        yield
        sib_left = pair(left, 2)
        sib_right.wait_recv()
        part[c_right, :, lanes] = part[c_right, :, lanes] + sib[1, :, lanes]
        right_lower = send(part.at[c_right, lower, lanes], from_left.at[lower, lanes], cols=c_right)
        sib_own = pair(x, 3)
        sib_left.wait_recv()
        part[c_left, :, lanes] = part[c_left, :, lanes] + sib[2, :, lanes]
        left_upper = send(part.at[c_left, upper, lanes], from_right.at[upper, lanes], cols=c_left)
        yield
        fwd_upper.wait_recv()
        part[c_right, upper, lanes] = part[c_right, upper, lanes] + fwd[upper, lanes]
        right_upper = send(part.at[c_right, upper, lanes], from_left.at[upper, lanes], cols=c_right)
        fwd_lower.wait_recv()
        part[c_left, lower, lanes] = part[c_left, lower, lanes] + fwd[lower, lanes]
        left_lower = send(part.at[c_left, lower, lanes], from_right.at[lower, lanes], cols=c_left)
        yield
        sib_own.wait_recv()
        total = part[c, :, lanes] + sib[3, :, lanes]
        for copy in (right_lower, left_upper, right_upper, left_lower):
            copy.wait_recv()
        got.append(total + from_left[:, lanes] + from_right[:, lanes])

    share = width // nz
    z_rows = pl.ds(pl.multiple_of(z * share, share), share)

    def p_parts(at):
        lanes = pl.ds(pl.multiple_of(at * block, block), block)
        return p_high[:, lanes], p_low[:, lanes]

    def reduced_and_applied(value, at):
        lanes = pl.ds(0, value.shape[1])
        own, zi, yi, to, ti, ia, za, xa = (b.at[at] for b in (az, z_in, y_in, t_out, t_in, i_all, z_all, x_all))
        own[:, lanes] = value
        send, arrive = net.group(zi.at[:, :, lanes])
        for d in range(1, nz):
            rows = pl.ds(pl.multiple_of(lax.rem(z + d, nz) * share, share), share)
            send(own.at[rows, lanes], zi.at[d - 1, :, lanes], rows=z_peer(d))
        yield
        total = own[z_rows, lanes]
        arrive()
        for d in range(1, nz):
            total = total + zi[d - 1, :, lanes]
        yi[y, :, lanes] = total
        if ny > 1:
            send, arrive = net.group(yi.at[pl.ds(0, ny - 1), :, lanes])
            for d in range(1, ny):
                send(yi.at[y, :, lanes], yi.at[y, :, lanes], rows=y_peer(d))
        yield
        if ny > 1:
            arrive()
        total = yi[0, :, lanes]
        for i in range(1, ny):
            total = total + yi[i, :, lanes]
        za[z_rows, lanes] = total
        total = total[:, :block]
        send, arrive = net.group(ti)
        for d in range(1, PEERS):
            to[c_peer(d)] = with_parts(total, p_parts(c_peer(d)), NN)
            send(to.at[c_peer(d)], ti.at[d - 1], cols=c_peer(d))
        send, got["summed"] = net.group(za.at[pl.ds(0, (nz - 1) * share), lanes])
        for d in range(1, nz):
            send(za.at[z_rows, lanes], za.at[z_rows, lanes], rows=z_peer(d))
        total = with_parts(total, p_parts(c), NN)
        yield
        arrive()
        for d in range(1, PEERS):
            total = total + ti[d - 1]
        ia[c] = total
        send, arrive = net.group(ia.at[pl.ds(0, PEERS - 1)])
        for d in range(1, PEERS):
            send(ia.at[c], ia.at[c], cols=c_peer(d))
        total = with_parts(total, p_parts(c), NT)
        yield
        arrive()
        for d in range(1, PEERS):
            source = lax.rem(c + PEERS - d, PEERS)
            total = total + with_parts(ia[source], p_parts(source), NT)
        xa[z_rows] = total
        send, arrive = net.group(xa.at[pl.ds(0, (nz - 1) * share)])
        for d in range(1, nz):
            send(xa.at[z_rows], xa.at[z_rows], rows=z_peer(d))
        yield
        arrive()

    def row_sum(twice, at):
        buffer = c_in.at[at]
        buffer[c] = packed(twice)
        send, arrive = net.group(buffer.at[pl.ds(0, PEERS - 1)])
        for d in range(1, PEERS):
            send(buffer.at[c], buffer.at[c], cols=c_peer(d))

        def end():
            arrive()
            total = buffer[0]
            for i in range(1, PEERS):
                total = total + buffer[i]
            return unpacked(total)

        return end

    def small_sum(value):
        piece = width // PEERS
        mine = pl.ds(pl.multiple_of(c * piece, piece), piece)
        sm_own[...] = value
        send, arrive = net.group(sm_x)
        for d in range(1, PEERS):
            rows = pl.ds(pl.multiple_of(c_peer(d) * piece, piece), piece)
            send(sm_own.at[rows], sm_x.at[d - 1], cols=c_peer(d))
        yield
        total = sm_own[mine]
        arrive()
        for d in range(1, PEERS):
            total = total + sm_x[d - 1]
        sm_z[z] = total
        send, arrive = net.group(sm_z.at[pl.ds(0, nz - 1)])
        for d in range(1, nz):
            send(sm_z.at[z], sm_z.at[z], rows=z_peer(d))
        yield
        arrive()
        total = sm_z[0]
        for i in range(1, nz):
            total = total + sm_z[i]
        sm_y[y] = total
        if ny > 1:
            send, arrive = net.group(sm_y.at[pl.ds(0, ny - 1)])
            for d in range(1, ny):
                send(sm_y.at[y], sm_y.at[y], rows=y_peer(d))
        yield
        if ny > 1:
            arrive()
        total = sm_y[0]
        for i in range(1, ny):
            total = total + sm_y[i]
        sm_out[mine] = total
        send, arrive = net.group(sm_out.at[pl.ds(0, width - piece)])
        for d in range(1, PEERS):
            send(sm_out.at[mine], sm_out.at[mine], cols=c_peer(d))
        yield
        arrive()

    def backward(full, lanes, sums, before=lambda at, step: None):
        def on_block(at, step):
            before(at, step)
            value = full[at, :, lanes]
            term = with_counts(value, counts[samples(at, lanes)], NN) * spread[at]
            term = term + jnp.sum(value, axis=1, keepdims=True) * lowest[at]
            sums.append(term if not sums else sums[-1] + term)

        return gather(full, lanes, on_block)

    def forward(value, lanes, at, got):
        def compute(j):
            at_lowest = jnp.sum(value * lowest[j], axis=1, keepdims=True)
            return with_counts(value * spread[j], counts[samples(j, lanes)], NT) + at_lowest

        return scatter(compute, lanes, *(b.at[at] for b in (y_part, y_sib, y_fwd, y_left, y_right)), got)

    def in_shares(value, at):
        for step, _ in enumerate(reduced_and_applied(value, at)):
            if step >= 4:
                fill(12)
        finish(work[0])
        return z_all[at], x_all[at]

    end_gram = row_sum(b_gram, 0)

    def load(step):
        at = order[step]
        loads[step].wait()
        g = g_f32[chunk(at)]
        low = jnp.min(g, axis=0, keepdims=True)
        width_of = jnp.max(g, axis=0, keepdims=True) - low
        one, two = low + 0.25 * width_of, low + 0.75 * width_of
        counts[chunk(at)] = jnp.where(g > two, 2.0, jnp.where(g > one, 1.0, 0.0)).astype(BF16)
        lowest[at] = low
        spread[at] = 0.5 * width_of

    def load_ahead(at, step):
        for later in ((0, 1, 2, 3), (4, 5), (6,), (7,))[step] if step < 4 else ():
            load(later)

    def orthonormal_first():
        got["summed"]()
        done = []
        yield from eliminate([with_identity(z_all[0, :, block:])], [False], done)
        got["two_l0_inv"], two_l0_t = factors(done[0])
        got["l0_inv"], got["l0_t"] = got["two_l0_inv"][:, :width], two_l0_t[:, :width]
        yield
        u_one[...] = exact(got["l0_inv"], b_own[...])

    totals = []
    finish(backward(b_full, whole, totals, load_ahead))
    work[0] = orthonormal_first()
    z_raw, x_raw = in_shares(jnp.concatenate([totals[-1], end_gram()], axis=1), 0)
    z_raw = z_raw[:, :block]

    def orthonormal_right():
        l0_inv = got["l0_inv"]
        z_one, x_one = exact(l0_inv, z_raw), exact(l0_inv, x_raw)
        end = row_sum(exact(z_one, doubled(x_one), NT), 1)
        yield
        done = []
        yield from eliminate([with_identity(end())], [False], done)
        two_l1_inv, got["two_l1_t"] = factors(done[0])
        got["l1_inv"], got["l1_t"] = two_l1_inv[:, :width], got["two_l1_t"][:, :width]
        got["left"] = side_by_side(exact(got["l1_inv"], got["two_l0_inv"]), -got["two_l1_t"])
        got["one"] = x_one, z_one

    work[0] = orthonormal_right()
    halves = []
    scatters = [forward(x_raw, lanes, 0, halves) for lanes in pieces]
    first, second = scatters[0], scatters[-1]
    fill(1)
    next(first)
    next(first)
    next(second)
    fill(3)
    next(first)
    next(second)
    fill(4)
    next(second)
    finish(work[0])
    l1_t = got["l1_t"]
    totals, gathers = [], []
    for lanes, steps in zip(pieces, scatters):
        finish(steps)
        n_full[c, :, lanes] = exact(got["left"], jnp.concatenate([halves[-1], u_one[:, lanes]], axis=0))
        gathers.append(backward(n_full, lanes, totals))
        next(gathers[-1])
    x_v, z_v = (exact(got["l1_inv"], v) for v in got["one"])
    for steps in gathers:
        next(steps)
    for steps in gathers:
        finish(steps)

    def first_target():
        got["summed"]()
        row, lane = iotas(width, width)
        unit = jnp.where(row == lane, 1.0, 0.0)
        got["target_t"] = exact(unit, exact(l1_t, got["l0_t"]), NT)
        yield

    def second_factors():
        end_h_one = row_sum(exact(x_w, doubled(z_v), NT), 2)
        yield
        h_one = end_h_one()
        h = h_one[:, :width]
        z_j, x_j = z_w - exact(h, z_v), x_w - exact(h, x_v)
        end_e = row_sum(exact(z_j, doubled(x_j), NT), 3)
        normal = exact(l1_t, doubled(l1_t), NT) + h_one
        yield
        done = []
        yield from eliminate([with_identity(h_one), with_identity(normal)], [False, True], done)
        two_l2_inv, two_l2_t = factors(done[0])
        l2_inv, l2_t = two_l2_inv[:, :width], two_l2_t[:, :width]
        s_inv = done[1][:, :width]
        yield
        left_c = exact(l2_inv, end_e()[:, :width])
        c_two = exact(left_c, doubled(l2_inv), NT)
        c_half = c_two[:, :width]
        got["l2_inv"] = l2_inv
        back_left = side_by_side(two_l2_t + exact(c_half, two_l2_inv), exact(l2_t, got["two_l1_t"]))
        back[...] = exact(back_left, jnp.concatenate([n_full[c], u_one[...]], axis=0))
        got["second"] = x_j, l2_inv, two_l2_t, s_inv, done[1], c_half, c_two

    def rest():
        x_j, l2_inv, two_l2_t, s_inv, s_full, c_half, c_two = got["second"]
        two_cross = exact(c_half, two_l2_t)
        cross = two_cross[:, :width]
        x_ref[0] = x_v
        x_ref[1] = exact(l2_inv, x_j)
        m_ref[1] = exact(c_half, c_two) - exact(exact(cross, s_inv), doubled(cross), NT)
        yield
        m_ref[2] = exact(exact(got["target_t"], s_inv), doubled(cross), NT)
        m_ref[3] = two_cross
        m_ref[4] = s_full
        m_ref[5] = doubled_lanes(got["target_t"])

    def doubled_lanes(value):
        row, lane = iotas(width, 2 * width)
        both = jnp.where(jnp.logical_or(lane == row, lane == row + width), 1.0, 0.0)
        return exact(value, both)

    work[0] = first_target()
    z_w, x_w = in_shares(totals[-1], 1)
    z_w = z_w[:, :block]
    work[0] = second_factors()
    halves = []
    scatters = [forward(x_w, lanes, 1, halves) for lanes in pieces]
    first, second = scatters[0], scatters[-1]
    fill(1)
    next(first)
    next(first)
    next(second)
    fill(2)
    next(first)
    next(second)
    fill(2)
    next(second)
    finish(work[0])
    n_gram = None
    for lanes, steps in zip(pieces, scatters):
        finish(steps)
        n_two = exact(got["l2_inv"], halves[-1]) - back[:, lanes]
        n_ref[:, lanes] = n_two
        term = exact(n_two, doubled(n_two), NT)
        n_gram = term if n_gram is None else n_gram + term
    work[0] = rest()
    for _ in small_sum(n_gram):
        fill(1)
    finish(work[0])
    m_ref[0] = sm_out[...]
    net.finish()


def last_block(n_ref, x_ref, m_ref, s_ref, u_ref):
    width = n_ref.shape[0]
    h_two = m_ref[0]
    done = []
    systems = [with_identity(h_two), with_identity(h_two + m_ref[1])]
    for _ in eliminate(systems, [False, True], done):
        pass
    l3_inv, _ = factors(done[0])
    u_ref[...] = exact(l3_inv[:, :width], n_ref[...])
    b_t = -exact(m_ref[2][:, :width], done[1][:, :width])
    a_t = exact(m_ref[5][:, :width] - exact(b_t, m_ref[3][:, :width]), m_ref[4][:, :width])
    s_ref[...] = SCALE * (exact(a_t, x_ref[0]) + exact(b_t, x_ref[1]))


def solution(mesh, ny=4):
    nrows = mesh.shape["rows"]
    nz = nrows // ny

    def per_device(genotypes, right_sides, inverse_r):
        rows, block = genotypes.shape
        rows_w, width = right_sides.shape
        variants = inverse_r.shape[1]
        half = width // 2
        share = width // nz
        piece = width // PEERS
        v = pltpu.VMEM
        any_space = pl.BlockSpec(memory_space=pl.ANY)
        vmem = pl.BlockSpec(memory_space=pltpu.VMEM)
        beside = block + 2 * width
        together = 2 * 6 + 4 + 4
        groups = together + 3 + 4
        arrivals = together + 3 * 13 + 4 * 10
        small = pl.pallas_call(
            functools.partial(body, nz, ny),
            out_shape=(
                jax.ShapeDtypeStruct((width, rows_w), F32),
                jax.ShapeDtypeStruct((2, width, block), F32),
                jax.ShapeDtypeStruct((6, width, 2 * width), F32),
            ),
            in_specs=[any_space] * 3,
            out_specs=[vmem] * 3,
            scratch_shapes=[
                v((rows, block), F32), v((width, rows_w), F32), v((block, variants), F32), v((rows, block), BF16),
                v((PEERS, 1, block), F32), v((PEERS, 1, block), F32),
                v((block, variants), BF16), v((block, variants), BF16),
                v((PEERS, width, rows_w), F32), v((PEERS, width, rows_w), F32),
                v((width, rows_w), F32), v((width, rows_w), F32),
                v((2, PEERS, width, rows_w), F32), v((2, CHIPS, width, rows_w), F32),
                v((2, width, rows_w), F32), v((2, width, rows_w), F32), v((2, width, rows_w), F32),
                v((2, width, beside), F32), v((2, nz - 1, share, beside), F32), v((2, ny, share, beside), F32),
                v((2, PEERS, share, block), F32), v((2, PEERS - 1, share, block), F32),
                v((2, PEERS, share, block), F32), v((2, width, beside), F32), v((2, width, block), F32),
                v((4, PEERS, half, 2 * width), F32),
                v((width, 2 * width), F32), v((PEERS - 1, piece, 2 * width), F32),
                v((nz, piece, 2 * width), F32), v((ny, piece, 2 * width), F32), v((width, 2 * width), F32),
                pltpu.SemaphoreType.DMA((PEERS + 2,)),
                pltpu.SemaphoreType.DMA((groups,)),
                pltpu.SemaphoreType.DMA((arrivals,)),
            ],
            compiler_params=pltpu.CompilerParams(
                collective_id=0, has_side_effects=True, vmem_limit_bytes=58 * 1024 * 1024
            ),
        )(genotypes, right_sides.T, inverse_r)
        s_t, u_t = pl.pallas_call(
            last_block,
            out_shape=(
                jax.ShapeDtypeStruct((width, block), F32),
                jax.ShapeDtypeStruct((width, rows_w), F32),
            ),
        )(*small)
        return s_t.T, u_t.T

    in_specs = (P("rows", "cols"), P(("rows", "cols"), None), P("cols", None))
    out_specs = (P("cols", None), P(("rows", "cols"), None))
    return jax.shard_map(
        per_device, mesh=mesh, in_specs=in_specs, out_specs=out_specs, check_vma=False
    )
```
